128 devices in a mesh: req: 8 (over z, x_hi), head: 16 (over x_lo, y, core).
Axes of the slice: x: 4 (x_hi: 2, x_lo: 2; x = x_hi * 2 + x_lo), y: 4, z: 4, core: 2. Of those that a mesh axis runs over, the one named last changes fastest.
Arguments:
- tokens: bfloat16 [8192, 2048], P(('req', 'head')), may hold values from -6 to 6
- in_gain: float32 [2, 2048], replicated, may hold values from 0.25 to 1.75
- w_query: bfloat16 [2, 2048, 2048], P(None, None, 'head'), may hold values from -0.125 to 0.125
- w_key: bfloat16 [2, 2048, 2048], P(None, None, 'head'), may hold values from -0.125 to 0.125
- w_value: bfloat16 [2, 2048, 4096], P(None, None, 'head'), may hold values from -0.125 to 0.125
- w_gate_z: bfloat16 [2, 2048, 4096], P(None, None, 'head'), may hold values from -0.125 to 0.125
- w_beta: bfloat16 [2, 2048, 32], P(None, None, 'head'), may hold values from -0.125 to 0.125
- w_decay: bfloat16 [2, 2048, 32], P(None, None, 'head'), may hold values from -0.125 to 0.125
- conv_query: float32 [2, 4, 2048], P(None, None, 'head'), may hold values from -3 to 3
- conv_key: float32 [2, 4, 2048], P(None, None, 'head'), may hold values from -3 to 3
- conv_value: float32 [2, 4, 4096], P(None, None, 'head'), may hold values from -3 to 3
- a_log: float32 [2, 32], P(None, 'head'), may hold values from -4 to 0.5
- dt_bias: float32 [2, 32], P(None, 'head'), may hold values from -4 to 0
- out_gain: float32 [2, 128], replicated, may hold values from 0.25 to 1.75
- w_out: bfloat16 [2, 4096, 2048], P(None, 'head'), may hold values from -0.09375 to 0.09375
- state_pool: float32 [32, 32, 128, 128], P('req', 'head'), may hold values from -6 to 6
- hit_owner: int32 [16, 2], P('req'), may hold values from 0 to 7, as said below
- hit_slot: int32 [16, 2], P('req'), may hold values from 0 to 3
- lengths: int32 [16], P('req'), may hold values from 1 to 512, as said below
Outputs:
- out_rows: bfloat16 [8192, 2048], P(('req', 'head'))
- final_states: float32 [16, 2, 32, 128, 128], P('req', None, 'head')
The draws below stay inside these ranges and needn't reach their ends.
Inputs may be any that keep to these rules, and one draw needn't show every extreme that they name: Request r's layer-l state is pool row hit_owner * 4 + hit_slot; every pool row is named by exactly one (request, layer); among the entries of the requests of one index of req at most 2 share an owner, and 2 do in every draw. `lengths`: some request has exactly 512 valid tokens.
All inputs are finite; a program needn't handle non-finite values.
Results may differ from the reference program's by a relative error of at most 0.025.
Values may be sent and summed in bfloat16 or wider, within the bound.
A program may use at most 128 MiB of HBM per device.

```python
import jax
import jax.numpy as jnp
from jax import lax

D = 2048
HV = 32
HK = 16
DK = 128
DV = 128
CONV = 4
L = 2
REQ_DEV = 2
BLOCK = 64
SUF = 512
SLOTS = 4
REQS = 16
TOKENS = 8192
N_REQ = 8
N_HEAD = 16


def hit_tables(key):
    base = jax.random.fold_in(key, 5)
    first, second, third, fourth = jax.random.split(base, 4)
    order = jax.random.permutation(first, N_REQ).astype(jnp.int32)
    coin = jax.random.randint(second, (), 0, 2)
    shifts = jnp.stack([order[0], order[0], order[1], jnp.where(coin == 1, order[2], order[1])])
    labels = jax.vmap(lambda sub: jax.random.permutation(sub, SLOTS))(jax.random.split(third, N_REQ)).astype(jnp.int32)
    places = jax.vmap(lambda sub: jax.random.permutation(sub, SLOTS))(jax.random.split(fourth, N_REQ)).astype(jnp.int32)
    target = jnp.arange(N_REQ, dtype=jnp.int32)[:, None]
    entry = jnp.broadcast_to(jnp.arange(SLOTS, dtype=jnp.int32)[None, :], (N_REQ, SLOTS))
    owners = (target + shifts[None, :]) % N_REQ
    slots = places[owners, entry]
    request = target * REQ_DEV + labels // L
    level = labels % L
    owner_table = jnp.zeros((REQS, L), jnp.int32).at[request, level].set(owners)
    slot_table = jnp.zeros((REQS, L), jnp.int32).at[request, level].set(slots)
    return (owner_table, slot_table)


def draw_hit_owner(key, part):
    owner_table, slot_table = hit_tables(key)
    return owner_table


def draw_hit_slot(key, part):
    owner_table, slot_table = hit_tables(key)
    return slot_table


def draw_lengths(key, part):
    key = jax.random.fold_in(key, 11)
    first, second = jax.random.split(key)
    drawn = jax.random.randint(first, (REQS,), 1, SUF + 1)
    longest = jax.random.randint(second, (), 0, REQS)
    return drawn.at[longest].set(SUF).astype(jnp.int32)


def block_scale(stream_key, extent, shards, least, largest):
    loudness, own = 1.0, jax.random.fold_in(stream_key, 6)
    for position, parts in shards:
        steps = jnp.exp(jax.random.uniform(jax.random.fold_in(own, position), (parts,), jnp.float32, least / len(shards), largest / len(shards)))
        loudness = loudness * jnp.repeat(steps, extent[position] // parts).reshape([-1 if axis == position else 1 for axis in range(len(extent))])
    return loudness


def gaussian(rng, dims, scale, bound, cuts=(), held_as=jnp.bfloat16):
    values = scale * jax.random.normal(rng, dims, jnp.float32)
    if cuts:
        values = values * block_scale(rng, dims, cuts, -0.22, 0.18)
    return jnp.clip(values, -bound, bound).astype(held_as)


def setup_inputs(seed: int = 0) -> dict:
    keys = jax.random.split(jax.random.key(seed), 20)
    return {
        "tokens": gaussian(keys[0], (TOKENS, D), 1.0, 6.0, ((0, 128),)),
        "in_gain": jnp.clip(1.0 + 0.15 * jax.random.normal(keys[1], (L, D), jnp.float32), 0.25, 1.75),
        "w_query": gaussian(keys[2], (L, D, HK * DK), D ** -0.5, 0.125, ((2, 16),)),
        "w_key": gaussian(keys[3], (L, D, HK * DK), D ** -0.5, 0.125, ((2, 16),)),
        "w_value": gaussian(keys[4], (L, D, HV * DV), D ** -0.5, 0.125, ((2, 16),)),
        "w_gate_z": gaussian(keys[5], (L, D, HV * DV), D ** -0.5, 0.125, ((2, 16),)),
        "w_beta": gaussian(keys[6], (L, D, HV), D ** -0.5, 0.125, ((2, 16),)),
        "w_decay": gaussian(keys[7], (L, D, HV), D ** -0.5, 0.125, ((2, 16),)),
        "conv_query": gaussian(keys[8], (L, CONV, HK * DK), 0.6, 3.0, ((2, 16),), jnp.float32),
        "conv_key": gaussian(keys[9], (L, CONV, HK * DK), 0.6, 3.0, ((2, 16),), jnp.float32),
        "conv_value": gaussian(keys[10], (L, CONV, HV * DV), 0.6, 3.0, ((2, 16),), jnp.float32),
        "a_log": jnp.clip(-4.0 + 4.5 * jax.random.uniform(keys[11], (L, HV), jnp.float32) ** block_scale(keys[11], (L, HV), ((1, 16),), -0.2, 0.2), -4.0, 0.5),
        "dt_bias": jnp.clip(-4.0 + 4.0 * jax.random.uniform(keys[12], (L, HV), jnp.float32) ** block_scale(keys[12], (L, HV), ((1, 16),), -0.2, 0.2), -4.0, 0.0),
        "out_gain": jnp.clip(1.0 + 0.15 * jax.random.normal(keys[13], (L, DV), jnp.float32), 0.25, 1.75),
        "w_out": gaussian(keys[14], (L, HV * DV, D), (HV * DV) ** -0.5, 0.09375, ((1, 16),)),
        "state_pool": gaussian(keys[15], (N_REQ * SLOTS, HV, DK, DV), 1.0, 6.0, ((0, 8), (1, 16)), jnp.float32),
        "hit_owner": draw_hit_owner(jax.random.fold_in(keys[19], 71), 0),
        "hit_slot": draw_hit_slot(jax.random.fold_in(keys[19], 71), 0),
        "lengths": draw_lengths(jax.random.fold_in(keys[19], 71), 0),
    }


EPS = 1e-06
PRECISE = lax.Precision.HIGHEST

def normalize(token_rows, gain):
    floats = token_rows.astype(jnp.float32)
    return floats * lax.rsqrt(lax.optimization_barrier(jnp.mean(floats * floats, -1, keepdims=True)) + EPS) * gain

def project(normed, weights):
    return jnp.concatenate([jnp.dot(normed, weight, preferred_element_type=jnp.float32) for weight in weights], 1)

def causal_conv(signal, kernel):
    kernel_taps = kernel.shape[0]
    length = signal.shape[1]
    padded = jnp.pad(signal, ((0, 0), (kernel_taps - 1, 0), (0, 0)))
    summed = padded[:, 0:length, :] * kernel[0]
    for offset in range(1, kernel_taps):
        summed = summed + padded[:, offset:offset + length, :] * kernel[offset]
    return summed

def unit_rows(vectors):
    return vectors * lax.rsqrt(lax.optimization_barrier(jnp.sum(vectors * vectors, -1, keepdims=True)) + EPS)

def unit_lower_inverse(strict_part):
    negated = -strict_part
    identity = jnp.eye(strict_part.shape[-1], dtype=jnp.float32)
    inverse = identity + negated
    power = negated
    for level in range(strict_part.shape[-1].bit_length() - 2):
        power = jnp.einsum('bnij,bnjk->bnik', power, power, precision=PRECISE)
        inverse = inverse + jnp.einsum('bnij,bnjk->bnik', inverse, power, precision=PRECISE)
    return inverse

def delta_blocks(queries, key_vecs, values, beta_gate, log_decay, state_init):
    batch, length, kdim = key_vecs.shape
    vdim = values.shape[2]
    blocks = length // BLOCK
    query_b = queries.reshape(batch, blocks, BLOCK, kdim)
    key_b = key_vecs.reshape(batch, blocks, BLOCK, kdim)
    value_b = values.reshape(batch, blocks, BLOCK, vdim)
    beta_b = beta_gate.reshape(batch, blocks, BLOCK)
    cumul = jnp.cumsum(log_decay.reshape(batch, blocks, BLOCK), -1)
    ranks = jnp.arange(BLOCK, dtype=jnp.int32)
    lower = ranks[:, None] >= ranks[None, :]
    strict = ranks[:, None] > ranks[None, :]
    spread = cumul[..., :, None] - cumul[..., None, :]
    decays = jnp.where(lower, jnp.exp(jnp.where(lower, spread, 0.0)), 0.0)
    key_dots = jnp.einsum('bnik,bnjk->bnij', key_b, key_b, precision=PRECISE)
    strict_part = jnp.where(strict, key_dots * decays * beta_b[..., :, None], 0.0)
    inverse = unit_lower_inverse(strict_part)
    right_side = jnp.concatenate([value_b * beta_b[..., None], key_b * (beta_b * jnp.exp(cumul))[..., None]], -1)
    solved = jnp.einsum('bnij,bnjc->bnic', inverse, right_side, precision=PRECISE)
    plain_part = solved[..., :vdim]
    state_part = solved[..., vdim:]
    mixing = jnp.einsum('bnik,bnjk->bnij', query_b, key_b, precision=PRECISE) * decays
    query_decay = query_b * jnp.exp(cumul)[..., None]
    key_tail = key_b * jnp.exp(cumul[..., -1:] - cumul)[..., None]
    tail_decay = jnp.exp(cumul[..., -1])

    def advance(state, pieces):
        plain_now, state_now, mixing_now, query_now, tail_keys, tail_now = pieces
        update = plain_now - jnp.einsum('bik,bkv->biv', state_now, state, precision=PRECISE)
        output = jnp.einsum('bik,bkv->biv', query_now, state, precision=PRECISE)
        output = output + jnp.einsum('bij,bjv->biv', mixing_now, update, precision=PRECISE)
        state = tail_now[:, None, None] * state + jnp.einsum('bik,biv->bkv', tail_keys, update, precision=PRECISE)
        return (state, output)
    moved = tuple((jnp.moveaxis(array, 1, 0) for array in (plain_part, state_part, mixing, query_decay, key_tail, tail_decay)))
    final, outputs = lax.scan(advance, state_init, moved)
    outputs = jnp.moveaxis(outputs, 0, 1).reshape(batch, length, vdim)
    return (outputs, final)

def mixer(projected, kernels, rates, head_gain, state_init, lengths, key_width, value_width):
    requests = lengths.shape[0]
    length = projected.shape[0] // requests
    key_heads = key_width // DK
    value_heads = value_width // DV
    cuts = [0, key_width, 2 * key_width, 2 * key_width + value_width, 2 * key_width + 2 * value_width, 2 * key_width + 2 * value_width + value_heads, 2 * key_width + 2 * value_width + 2 * value_heads]
    pieces = [projected[:, cuts[part]:cuts[part + 1]].reshape(requests, length, cuts[part + 1] - cuts[part]) for part in range(6)]
    queries = jax.nn.silu(causal_conv(pieces[0], kernels[0])).reshape(requests, length, key_heads, DK)
    queries = unit_rows(queries) * DK ** (-0.5)
    key_vecs = unit_rows(jax.nn.silu(causal_conv(pieces[1], kernels[1])).reshape(requests, length, key_heads, DK))
    values = jax.nn.silu(causal_conv(pieces[2], kernels[2])).reshape(requests, length, value_heads, DV)
    gate_z = pieces[3].reshape(requests, length, value_heads, DV)
    positions = jnp.arange(length, dtype=jnp.int32)
    valid = positions[None, :] < lengths[:, None]
    beta_gate = jnp.where(valid[..., None], jax.nn.sigmoid(pieces[4]), 0.0)
    log_decay = jnp.where(valid[..., None], -jnp.exp(rates[0]) * jax.nn.softplus(pieces[5] + rates[1]), 0.0)
    queries = jnp.repeat(queries, value_heads // key_heads, axis=2)
    key_vecs = jnp.repeat(key_vecs, value_heads // key_heads, axis=2)

    def flatten(array):
        return jnp.moveaxis(array, 2, 1).reshape(requests * value_heads, length, array.shape[3])

    def flatten_gate(array):
        return jnp.moveaxis(array, 2, 1).reshape(requests * value_heads, length)
    outputs, final = delta_blocks(flatten(queries), flatten(key_vecs), flatten(values), flatten_gate(beta_gate), flatten_gate(log_decay), state_init.reshape(requests * value_heads, DK, DV))
    outputs = jnp.moveaxis(outputs.reshape(requests, value_heads, length, DV), 1, 2)
    scaled = outputs * lax.rsqrt(lax.optimization_barrier(jnp.mean(outputs * outputs, -1, keepdims=True)) + EPS) * head_gain
    scaled = scaled * jax.nn.silu(gate_z) * valid[..., None, None].astype(jnp.float32)
    return (scaled.reshape(requests * length, value_heads * DV).astype(jnp.bfloat16), final.reshape(requests, value_heads, DK, DV))

def reference(tokens, in_gain, w_query, w_key, w_value, w_gate_z, w_beta, w_decay, conv_query, conv_key, conv_value, a_log, dt_bias, out_gain, w_out, state_pool, hit_owner, hit_slot, lengths):
    starts = state_pool[(hit_owner * SLOTS + hit_slot).astype(jnp.int32)]
    token_rows = tokens.reshape(REQS, SUF, D)
    group_width = HV * DV // N_HEAD
    finals = []
    for layer_index in range(L):
        weights = (w_query[layer_index], w_key[layer_index], w_value[layer_index], w_gate_z[layer_index], w_beta[layer_index], w_decay[layer_index])
        kernels = (conv_query[layer_index], conv_key[layer_index], conv_value[layer_index])
        rates = (a_log[layer_index], dt_bias[layer_index])
        out_weight = w_out[layer_index]

        def one_request(item):
            rows_one, length_one, state_one = item
            normed = normalize(rows_one, in_gain[layer_index]).astype(jnp.bfloat16)
            projected = project(normed, weights)
            mixed, final = mixer(projected, kernels, rates, out_gain[layer_index], state_one[None], length_one[None], HK * DK, HV * DV)

            def add_group(summed, group):
                piece = lax.dynamic_slice_in_dim(mixed, group * group_width, group_width, 1)
                rows_w = lax.dynamic_slice_in_dim(out_weight, group * group_width, group_width, 0)
                part_sum = jnp.dot(piece, rows_w, preferred_element_type=jnp.float32).astype(jnp.bfloat16)
                return (summed + lax.optimization_barrier(part_sum).astype(jnp.float32), None)
            branch, unused = lax.scan(add_group, jnp.zeros((SUF, D), jnp.float32), jnp.arange(N_HEAD, dtype=jnp.int32))
            return ((rows_one.astype(jnp.float32) + branch).astype(jnp.bfloat16), final[0])
        token_rows, final = lax.map(one_request, (token_rows, lengths, starts[:, layer_index]))
        finals.append(final)
    return (token_rows.reshape(REQS * SUF, D), jnp.stack(finals, 1))
```

```python
import jax
import jax.numpy as jnp
from jax import lax
from jax.experimental import pallas as pl
from jax.experimental.pallas import tpu as pltpu
from jax.sharding import PartitionSpec as P

DK = 128
DV = 128
L = 2
SLOTS = 4
SUF = 512
CONV = 4
HEADS = 2
CHUNK = 128
BLOCKS = SUF // CHUNK
PAD = 8
EPS = 1e-06
BF = jnp.bfloat16
F32 = jnp.float32
PRECISE = lax.Precision.HIGHEST


def silu(v):
    return v / (1.0 + jnp.exp(-v))


def conv_block(ref, row, width, taps, tap_col):
    window = ref[pl.ds(row, CHUNK + PAD), 0:width]
    total = None
    for tap in range(CONV):
        first = PAD - (CONV - 1) + tap
        term = window[first : first + CHUNK] * taps[tap : tap + 1, tap_col : tap_col + width]
        total = term if total is None else total + term
    return silu(total)


def unit_rows(vectors):
    return vectors * lax.rsqrt(jnp.sum(vectors * vectors, -1, keepdims=True) + EPS)


def mm(a, b):
    return jnp.dot(a.astype(BF), b.astype(BF), preferred_element_type=F32)


def nt(a, b):
    return lax.dot_general(
        a.astype(BF), b.astype(BF), (((1,), (1,)), ((), ())), preferred_element_type=F32
    )


def lower_inverse(strict, rows, cols):
    size = 16
    diag = jnp.where(rows // size == cols // size, -strict, 0.0)
    inverse = jnp.where(rows == cols, 1.0, 0.0) + diag
    power = mm(diag, diag)
    for _ in range(2):
        both = mm(jnp.concatenate([power, inverse], 0), power)
        inverse = inverse + both[CHUNK:]
        power = both[:CHUNK]
    inverse = inverse + mm(inverse, power)
    while size < CHUNK:
        joined = (rows // (2 * size) == cols // (2 * size)) & (rows // size > cols // size)
        corner = jnp.where(joined, strict, 0.0)
        inverse = inverse - mm(inverse, mm(corner, inverse))
        size *= 2
    return inverse


def gate_rows(raw, a_log, dt_bias, length):
    valid = lax.broadcasted_iota(jnp.int32, (1, SUF), 1) < length
    rows = []
    for head in range(HEADS):
        rows.append(jnp.where(valid, 1.0 / (1.0 + jnp.exp(-raw[head : head + 1])), 0.0))
    for head in range(HEADS):
        shifted = raw[HEADS + head : HEADS + head + 1] + dt_bias[head]
        soft = jnp.maximum(shifted, 0.0) + jnp.log1p(jnp.exp(-jnp.abs(shifted)))
        rate = jnp.exp(jnp.full((1, SUF), a_log[head], F32))
        rows.append(jnp.where(valid, -rate * soft, 0.0))
    rows.append(jnp.zeros((8 - 2 * HEADS, SUF), F32))
    return jnp.concatenate(rows, 0)


def block_terms(block, q_ref, k_ref, v_ref, taps, gates, move_ref, add_ref, tail_ref):
    row = block * CHUNK
    rows = lax.broadcasted_iota(jnp.int32, (CHUNK, CHUNK), 0)
    cols = lax.broadcasted_iota(jnp.int32, (CHUNK, CHUNK), 1)
    upper = jnp.where(rows <= cols, 1.0, 0.0)
    sums = jnp.dot(gates, upper, precision=lax.Precision.HIGHEST, preferred_element_type=F32)
    columns = jnp.concatenate([gates, sums], 0).T
    queries = unit_rows(conv_block(q_ref, row, DK, taps, 0)) * DK ** (-0.5)
    keys = unit_rows(conv_block(k_ref, row, DK, taps, DK))
    values = conv_block(v_ref, row, HEADS * DV, taps, 2 * DK)
    dots = nt(jnp.concatenate([keys, queries], 0), keys)
    for head in range(HEADS):
        beta = columns[:, head : head + 1]
        cumul = columns[:, 8 + HEADS + head : 9 + HEADS + head]
        cumul_row = sums[HEADS + head : HEADS + head + 1]
        last = cumul[CHUNK - 1 :]
        decays = jnp.where(
            rows >= cols, jnp.exp(jnp.minimum(cumul - cumul_row, 0.0)), 0.0
        )
        strict = jnp.where(rows > cols, dots[:CHUNK] * decays * beta, 0.0)
        inverse = lower_inverse(strict, rows, cols)
        grown = jnp.exp(cumul)
        right = jnp.concatenate(
            [values[:, head * DV : (head + 1) * DV] * beta, keys * (beta * grown)], 1
        )
        solved = mm(inverse, right)
        key_tail = keys * jnp.exp(last - cumul)
        mixing = dots[CHUNK:] * decays
        both = mm(jnp.concatenate([key_tail.T, mixing], 0), solved)
        move = jnp.concatenate([-both[:DK, DV:], queries * grown - both[DK:, DV:]], 0)
        move_ref[block, head] = move.astype(BF)
        add_ref[block, head] = both[:, :DV]
        tail_ref[block, head] = jnp.broadcast_to(jnp.exp(last), (8, DV))


def run_states(start, move_ref, add_ref, tail_ref, z_ref, gain, length, store):
    states = [start[head] for head in range(HEADS)]
    for block in range(BLOCKS):
        place = block * CHUNK + lax.broadcasted_iota(jnp.int32, (CHUNK, 1), 0)
        valid = (place < length).astype(F32)
        for head in range(HEADS):
            result = mm(move_ref[block, head], states[head]) + add_ref[block, head]
            states[head] = tail_ref[block, head][0:1] * states[head] + result[:DK]
            out = result[DK:]
            scale = lax.rsqrt(jnp.mean(out * out, -1, keepdims=True) + EPS)
            gate = z_ref[pl.ds(block * CHUNK + PAD, CHUNK), head * DV : (head + 1) * DV]
            store(block, head, (out * scale * gain * silu(gate) * valid).astype(BF))
    return states


def mixer_kernel(
    q_in, k_in, v_in, z_in, raw, taps, a_log, dt_bias, lengths, gain, start,
    mixed, final, q_ref, k_ref, v_ref, z_ref, move_ref, add_ref, tail_ref,
):
    request = pl.program_id(0)
    length = lengths[request]
    for source, target in ((q_in, q_ref), (k_in, k_ref), (v_in, v_ref), (z_in, z_ref)):
        target[0:PAD] = jnp.zeros((PAD, target.shape[1]), F32)
        target[PAD:] = source[...]
    gates = gate_rows(raw[...], a_log, dt_bias, length)
    tap_rows = taps[...]
    for block in range(BLOCKS):
        block_terms(
            block, q_ref, k_ref, v_ref, tap_rows,
            gates[:, block * CHUNK : (block + 1) * CHUNK], move_ref, add_ref, tail_ref,
        )

    def store(block, head, rows):
        mixed[pl.ds(block * CHUNK, CHUNK), head * DV : (head + 1) * DV] = rows

    states = run_states(
        [start[0, head] for head in range(HEADS)],
        move_ref, add_ref, tail_ref, z_ref, gain[...], length, store,
    )
    for head in range(HEADS):
        final[0, head] = states[head]


def mixer(q, k, v, z, raw, taps, a_log, dt_bias, lengths, gain, start):
    requests = lengths.shape[0]
    smem = pl.BlockSpec(memory_space=pltpu.SMEM)

    def rows(width):
        return pl.BlockSpec((SUF, width), lambda r: (r, 0))

    return pl.pallas_call(
        mixer_kernel,
        grid=(requests,),
        in_specs=[
            rows(DK), rows(DK), rows(HEADS * DV), rows(HEADS * DV),
            pl.BlockSpec((2 * HEADS, SUF), lambda r: (0, r)),
            pl.BlockSpec((CONV, 2 * DK + HEADS * DV), lambda r: (0, 0)),
            smem, smem, smem,
            pl.BlockSpec((1, DV), lambda r: (0, 0)),
            pl.BlockSpec((1, HEADS, DK, DV), lambda r: (r, 0, 0, 0)),
        ],
        out_specs=[
            rows(HEADS * DV),
            pl.BlockSpec((1, HEADS, DK, DV), lambda r: (r, 0, 0, 0)),
        ],
        out_shape=[
            jax.ShapeDtypeStruct((requests * SUF, HEADS * DV), BF),
            jax.ShapeDtypeStruct((requests, HEADS, DK, DV), F32),
        ],
        scratch_shapes=[
            pltpu.VMEM((PAD + SUF, DK), F32),
            pltpu.VMEM((PAD + SUF, DK), F32),
            pltpu.VMEM((PAD + SUF, HEADS * DV), F32),
            pltpu.VMEM((PAD + SUF, HEADS * DV), F32),
            pltpu.VMEM((BLOCKS, HEADS, 2 * CHUNK, DK), BF),
            pltpu.VMEM((BLOCKS, HEADS, 2 * CHUNK, DV), F32),
            pltpu.VMEM((BLOCKS, HEADS, 8, DV), F32),
        ],
        compiler_params=pltpu.CompilerParams(vmem_limit_bytes=48 * 1024 * 1024),
        cost_estimate=pl.CostEstimate(flops=2 * 10**9, bytes_accessed=8 * 10**6, transcendentals=10**6),
    )(q, k, v, z, raw, taps, a_log, dt_bias, lengths, gain, start)


def normalize(token_rows, gain):
    floats = token_rows.astype(F32)
    return floats * lax.rsqrt(jnp.mean(floats * floats, -1, keepdims=True) + EPS) * gain


def on_device(
    tokens, in_gain, w_query, w_key, w_value, w_gate_z, w_beta, w_decay,
    conv_query, conv_key, conv_value, a_log, dt_bias, out_gain, w_out,
    state_pool, hit_owner, hit_slot, lengths,
):
    requests = lengths.shape[0]
    head_count = state_pool.shape[1]
    wanted = (hit_owner * SLOTS + hit_slot).reshape(-1)
    piece = lax.all_gather(state_pool.astype(BF), "req", axis=0, tiled=True)
    starts = piece[wanted].astype(F32).reshape(requests, L, head_count, DK, DV)

    def dot(a, b):
        return jnp.dot(a, b, preferred_element_type=F32)

    def branch(rows_in, level):
        normed = normalize(rows_in, in_gain[level]).astype(BF)
        everyone = lax.all_gather(normed, "head", axis=0, tiled=True)
        small = jnp.concatenate([w_beta[level], w_decay[level]], 1)
        raw = lax.dot_general(small, everyone, (((0,), (1,)), ((), ())), preferred_element_type=F32)
        taps = jnp.concatenate([conv_query[level], conv_key[level], conv_value[level]], 1)
        mixed, final = mixer(
            dot(everyone, w_query[level]), dot(everyone, w_key[level]),
            dot(everyone, w_value[level]), dot(everyone, w_gate_z[level]),
            raw, taps, a_log[level], dt_bias[level], lengths, out_gain[level : level + 1],
            starts[:, level],
        )
        added = lax.psum_scatter(
            dot(mixed, w_out[level]).astype(BF), "head", scatter_dimension=0, tiled=True
        ).astype(F32)
        return (rows_in.astype(F32) + added).astype(BF), final

    current, first_end = branch(tokens, 0)
    result, second_end = branch(current, 1)
    return (result, jnp.stack([first_end, second_end], 1))


def solution(mesh):
    heads = P(None, None, "head")
    in_specs = (
        P(("req", "head"), None), P(), heads, heads, heads, heads, heads, heads,
        heads, heads, heads, P(None, "head"), P(None, "head"), P(),
        P(None, "head", None), P("req", "head", None, None),
        P("req", None), P("req", None), P("req"),
    )
    out_specs = (P(("req", "head"), None), P("req", None, "head", None, None))
    return jax.shard_map(
        on_device, mesh=mesh, in_specs=in_specs, out_specs=out_specs, check_vma=False
    )
```

```python
import jax
import jax.numpy as jnp
from jax import lax
from jax.experimental import pallas as pl
from jax.experimental.pallas import tpu as pltpu
from jax.sharding import PartitionSpec as P

DK = 128
DV = 128
L = 2
SLOTS = 4
SUF = 512
CONV = 4
HEADS = 2
CHUNK = 128
BLOCKS = SUF // CHUNK
PAD = 8
EPS = 1e-06
BF = jnp.bfloat16
F32 = jnp.float32
D = 2048
ROWS = 64
PIECE = 16
PIECES = ROWS // PIECE
WIDE = 2 * DK + 2 * HEADS * DV
SEMS = 176


def silu(v):
    return v / (1.0 + jnp.exp(-v))


def conv_block(ref, row, width, taps):
    window = ref[pl.ds(row, CHUNK + PAD), 0:width]
    total = None
    for tap in range(CONV):
        first = PAD - (CONV - 1) + tap
        term = window[first : first + CHUNK] * taps[tap : tap + 1]
        total = term if total is None else total + term
    return silu(total)


def unit_rows(vectors):
    return vectors * lax.rsqrt(jnp.sum(vectors * vectors, -1, keepdims=True) + EPS)


def mm(a, b):
    return jnp.dot(a.astype(BF), b.astype(BF), preferred_element_type=F32)


def nt(a, b):
    return lax.dot_general(
        a.astype(BF), b.astype(BF), (((1,), (1,)), ((), ())), preferred_element_type=F32
    )


def lower_inverses(stricts, rows, cols):
    size = 16
    near = rows // size == cols // size
    eye = jnp.where(rows == cols, 1.0, 0.0)
    diags = [jnp.where(near, -strict, 0.0) for strict in stricts]
    inverses = [eye + diag for diag in diags]
    powers = [mm(diag, diag) for diag in diags]
    for _ in range(2):
        both = [
            mm(jnp.concatenate([power, inverse], 0), power)
            for power, inverse in zip(powers, inverses)
        ]
        inverses = [inverse + pair[CHUNK:] for inverse, pair in zip(inverses, both)]
        powers = [pair[:CHUNK] for pair in both]
    inverses = [inverse + mm(inverse, power) for inverse, power in zip(inverses, powers)]
    while size < CHUNK:
        joined = (rows // (2 * size) == cols // (2 * size)) & (rows // size > cols // size)
        halves = [
            mm(jnp.where(joined, strict, 0.0), inverse)
            for strict, inverse in zip(stricts, inverses)
        ]
        inverses = [inverse - mm(inverse, half) for inverse, half in zip(inverses, halves)]
        size *= 2
    return inverses


def gate_rows(raw, a_log, dt_bias, valid):
    rows = []
    for head in range(HEADS):
        rows.append(jnp.where(valid, 1.0 / (1.0 + jnp.exp(-raw[head : head + 1])), 0.0))
    for head in range(HEADS):
        shifted = raw[HEADS + head : HEADS + head + 1] + dt_bias[head]
        soft = jnp.maximum(shifted, 0.0) + jnp.log1p(jnp.exp(-jnp.abs(shifted)))
        rate = jnp.exp(jnp.full((1, CHUNK), a_log[head], F32))
        rows.append(jnp.where(valid, -rate * soft, 0.0))
    rows.append(jnp.zeros((8 - 2 * HEADS, CHUNK), F32))
    return jnp.concatenate(rows, 0)


def block_terms(blocks, q_ref, k_ref, v_ref, raws, taps, a_log, dt_bias, length, move_ref, add_ref, tail_ref):
    rows = lax.broadcasted_iota(jnp.int32, (CHUNK, CHUNK), 0)
    cols = lax.broadcasted_iota(jnp.int32, (CHUNK, CHUNK), 1)
    lane = lax.broadcasted_iota(jnp.int32, (1, CHUNK), 1)
    upper = jnp.where(rows <= cols, 1.0, 0.0)
    gates = [
        gate_rows(raw, a_log, dt_bias, block * CHUNK + lane < length)
        for block, raw in zip(blocks, raws)
    ]
    sums = jnp.dot(
        jnp.concatenate(gates, 0), upper, precision=lax.Precision.HIGHEST, preferred_element_type=F32
    )
    sums = [sums[8 * index : 8 * index + 8] for index in range(len(blocks))]
    columns = [jnp.concatenate([gate, total], 0).T for gate, total in zip(gates, sums)]
    keys = [unit_rows(conv_block(k_ref, block * CHUNK, DK, taps[1])) for block in blocks]
    queries = [
        unit_rows(conv_block(q_ref, block * CHUNK, DK, taps[0])) * DK ** (-0.5) for block in blocks
    ]
    dots = [nt(jnp.concatenate([key, query], 0), key) for key, query in zip(keys, queries)]
    units = [(index, head) for index in range(len(blocks)) for head in range(HEADS)]
    stricts, decays = [], []
    for index, head in units:
        cumul = columns[index][:, 8 + HEADS + head : 9 + HEADS + head]
        cumul_row = sums[index][HEADS + head : HEADS + head + 1]
        decay = jnp.where(rows >= cols, jnp.exp(jnp.minimum(cumul - cumul_row, 0.0)), 0.0)
        beta = columns[index][:, head : head + 1]
        stricts.append(jnp.where(rows > cols, dots[index][:CHUNK] * decay * beta, 0.0))
        decays.append(decay)
    inverses = lower_inverses(stricts, rows, cols)
    values = [conv_block(v_ref, block * CHUNK, HEADS * DV, taps[2]) for block in blocks]
    solved = []
    for (index, head), inverse in zip(units, inverses):
        beta = columns[index][:, head : head + 1]
        grown = jnp.exp(columns[index][:, 8 + HEADS + head : 9 + HEADS + head])
        right = jnp.concatenate(
            [values[index][:, head * DV : (head + 1) * DV] * beta, keys[index] * (beta * grown)], 1
        )
        solved.append(mm(inverse, right))
    for (index, head), decay, solution_now in zip(units, decays, solved):
        cumul = columns[index][:, 8 + HEADS + head : 9 + HEADS + head]
        last = cumul[CHUNK - 1 :]
        key_tail = keys[index] * jnp.exp(last - cumul)
        mixing = dots[index][CHUNK:] * decay
        both = mm(jnp.concatenate([key_tail.T, mixing], 0), solution_now)
        move = jnp.concatenate(
            [-both[:DK, DV:], queries[index] * jnp.exp(cumul) - both[DK:, DV:]], 0
        )
        move_ref[blocks[index], head] = move.astype(BF)
        add_ref[blocks[index], head] = both[:, :DV]
        tail_ref[blocks[index], head] = jnp.broadcast_to(jnp.exp(last), (8, DV))


def run_states(start, move_ref, add_ref, tail_ref, z_ref, gain, length, store):
    states = [start[head] for head in range(HEADS)]
    for block in range(BLOCKS):
        place = block * CHUNK + lax.broadcasted_iota(jnp.int32, (CHUNK, 1), 0)
        valid = (place < length).astype(F32)
        results = [
            mm(move_ref[block, head], states[head]) + add_ref[block, head] for head in range(HEADS)
        ]
        for head in range(HEADS):
            states[head] = tail_ref[block, head][0:1] * states[head] + results[head][:DK]
            out = results[head][DK:]
            scale = lax.rsqrt(jnp.mean(out * out, -1, keepdims=True) + EPS)
            gate = z_ref[pl.ds(block * CHUNK, CHUNK), head * DV : (head + 1) * DV]
            store(block, head, (out * scale * gain * silu(gate) * valid).astype(BF))
    return states


def spot(x, y, core):
    return x * 8 + y * 2 + core


def piece(index):
    return pl.ds(index * PIECE, PIECE)


def layers_kernel(
    tokens, in_gain, w_query, w_key, w_value, w_gate, w_beta, w_decay,
    conv_query, conv_key, conv_value, a_log, dt_bias, out_gain, w_out,
    pool, owner, slot, lengths, wanted,
    out_rows, final,
    weights, outs, buf, q_ref, k_ref, v_ref, z_ref, raw_ref, move_ref, add_ref, tail_ref,
    mixed, stage, sib, land, last_land, held, current, pool_in, zbuf, xsend, xland,
    table_in, table, send_sems, recv_sems, local_sems,
):
    me = lax.axis_index("head")
    group = lax.axis_index("req")
    x, y, core = me // 8, (me // 2) % 4, me % 2
    z, high = group // 2, group % 2
    other, up, down, far = 1 - x, (y + 1) % 4, (y + 3) % 4, (y + 2) % 4

    def plane(a, b):
        return spot(a, b, core)

    to_x, to_up, to_down = ({"head": plane(other, y)}, {"head": plane(x, up)}, {"head": plane(x, down)})
    sibling = {"head": spot(x, y, 1 - core)}
    to_high = {"req": z * 2 + 1 - high}
    to_z = [{"req": ((z + step) % 4) * 2 + high} for step in (1, 3, 2)]

    copies = []

    def send(source, target, device):
        index = len(copies)
        copy = pltpu.make_async_remote_copy(
            src_ref=source,
            dst_ref=target,
            send_sem=send_sems.at[index],
            recv_sem=recv_sems.at[index],
            device_id=device,
            device_id_type=pl.DeviceIdType.MESH,
        )
        copy.start()
        copies.append(copy)
        return copy

    loads = []

    def load(source, target):
        copy = pltpu.make_async_copy(source, target, local_sems.at[len(loads)])
        copy.start()
        loads.append(copy)
        return copy

    pool_load = load(pool, pool_in)
    weight_loads, out_loads = [], []
    for level in range(L):
        first = 0
        mine = []
        for source, width in (
            (w_query, DK), (w_key, DK), (w_value, HEADS * DV), (w_gate, HEADS * DV),
        ):
            mine.append(
                load(source.at[level], weights.at[level, :, pl.ds(first, width)])
            )
            first += width
        weight_loads.append(mine)
        out_loads.append(load(w_out.at[level], outs.at[level]))

    barrier = pltpu.get_barrier_semaphore()
    partners = [to_x, to_up, to_down, sibling, to_high] + to_z
    for partner in partners:
        pl.semaphore_signal(
            barrier, inc=1, device_id=partner, device_id_type=pl.DeviceIdType.MESH
        )
    pl.semaphore_wait(barrier, len(partners))

    current[...] = tokens[...]
    for ref in (q_ref, k_ref, v_ref):
        ref[:, 0:PAD] = jnp.zeros((2, PAD, ref.shape[2]), F32)

    def small_weights(level):
        rows = jnp.concatenate(
            [
                w_beta[level].astype(F32),
                w_decay[level].astype(F32),
                jnp.zeros((128 - 2 * HEADS, D), F32),
            ],
            0,
        )
        weights[level, :, WIDE:] = rows.T.astype(BF)

    def gather_start(level):
        floats = current[...].astype(F32)
        scale = lax.rsqrt(jnp.mean(floats * floats, -1, keepdims=True) + EPS)
        buf[level, me] = (floats * scale * in_gain[level : level + 1]).astype(BF)
        parts = {"x1": [], "p1": [], "m1": []}
        for p in range(PIECES):
            ref = buf.at[level, me, piece(p)]
            parts["p1"].append(send(ref, ref, to_up))
            parts["m1"].append(send(ref, ref, to_down))
            parts["x1"].append(send(ref, ref, to_x))
        parts["own"] = send(buf.at[level, me], buf.at[level, me], sibling)
        return parts

    def pass_block(level, block, rows=None):
        ref = buf.at[level, block] if rows is None else buf.at[level, block, rows]
        return send(ref, ref, sibling)

    def pass_piece(level, block, p, device):
        ref = buf.at[level, block, piece(p)]
        return send(ref, ref, device)

    def gather_near(level, parts):
        parts["p2"], parts["m2"], parts["p3"], parts["m3"] = [], [], [], []
        for p in range(PIECES):
            parts["p1"][p].wait_recv()
            if p < PIECES // 2:
                parts["p2"].append(pass_piece(level, plane(x, down), p, to_up))
            parts["m1"][p].wait_recv()
            if p >= PIECES // 2:
                parts["m2"].append(pass_piece(level, plane(x, up), p, to_down))
            parts["x1"][p].wait_recv()
            parts["p3"].append(pass_piece(level, plane(other, y), p, to_up))
            parts["m3"].append(pass_piece(level, plane(other, y), p, to_down))
        parts["down"] = pass_block(level, plane(x, down))
        parts["up"] = pass_block(level, plane(x, up))
        parts["across"] = pass_block(level, plane(other, y))

    def gather_far(level, parts):
        half = PIECES // 2
        parts["x2"] = []
        block = plane(x, far)
        for p in range(half):
            parts["p2"][p].wait_recv()
            parts["x2"].append(pass_piece(level, block, p, to_x))
        parts["far1"] = pass_block(level, block, pl.ds(0, ROWS // 2))
        for p in range(half):
            parts["m2"][p].wait_recv()
            parts["x2"].append(pass_piece(level, block, half + p, to_x))
        parts["far2"] = pass_block(level, block, pl.ds(ROWS // 2, ROWS // 2))

    def gather_rest(level, parts):
        for name, place in (("p3", down), ("m3", up), ("x2", far)):
            for copy in parts[name]:
                copy.wait_recv()
            parts[name + "s"] = pass_block(level, plane(other, place))

    def keep(level, request, result, row, count):
        place = pl.ds(row + PAD, count)
        q_ref[request, place] = result[:, 0:DK]
        k_ref[request, place] = result[:, DK : 2 * DK]
        v_ref[request, place] = result[:, 2 * DK : 2 * DK + HEADS * DV]
        z_ref[request, pl.ds(row, count)] = result[:, 2 * DK + HEADS * DV : WIDE]
        raw_ref[request, pl.ds(row, count)] = result[:, WIDE:]

    def project_chunk(level, b):
        rows = buf[level, pl.ds(spot(x, b, 0), 2)].reshape(CHUNK, D)
        result = jnp.dot(rows, weights[level], preferred_element_type=F32)
        keep(level, x, result, pl.multiple_of(b * CHUNK, CHUNK), CHUNK)

    def project_request(level, request):
        rows = buf[level, pl.ds(request * 8, 8)].reshape(SUF, D)
        result = jnp.dot(rows, weights[level], preferred_element_type=F32)
        keep(level, request, result, 0, SUF)

    def mix_blocks(level, request):
        blocks = list(range(BLOCKS))
        raws = [
            raw_ref[request, pl.ds(block * CHUNK, CHUNK)].T[0 : 2 * HEADS] for block in blocks
        ]
        block_terms(
            blocks, q_ref.at[request], k_ref.at[request], v_ref.at[request], raws,
            (conv_query[level], conv_key[level], conv_value[level]),
            [a_log[level, head] for head in range(HEADS)],
            [dt_bias[level, head] for head in range(HEADS)],
            lengths[request], move_ref, add_ref, tail_ref,
        )

    def mix_states(level, request):
        holder = owner[request, level]
        near = zbuf[(holder // 2) * SLOTS + slot[request, level]]
        start = jnp.where(holder % 2 == high, near, xland[request * L + level]).astype(F32)

        def store(block, head, rows):
            mixed[pl.ds(block * CHUNK, CHUNK), head * DV : (head + 1) * DV] = rows

        states = run_states(
            start, move_ref, add_ref, tail_ref, z_ref.at[request], out_gain[level : level + 1],
            lengths[request], store,
        )
        for head in range(HEADS):
            final[request, level, head] = states[head]

    def kept(level, half, index, p):
        row = pl.multiple_of(core * ROWS + p * PIECE, PIECE)
        mine = stage[level, half, index, pl.ds(row, PIECE)].astype(F32)
        return mine + sib[level, half, index, piece(p)].astype(F32)

    def scatter_start(level, half):
        pairs = []
        for index, b in enumerate((far, down, up, y)):
            rows = mixed[pl.ds(pl.multiple_of(b * CHUNK, CHUNK), CHUNK)]
            stage[level, half, index] = jnp.dot(
                rows, outs[level], preferred_element_type=F32
            ).astype(BF)
            theirs = pl.ds(pl.multiple_of((1 - core) * ROWS, ROWS), ROWS)
            pairs.append(send(stage.at[level, half, index, theirs], sib.at[level, half, index], sibling))
        middle = PIECES // 2
        todo = {"pairs": pairs, "b": [None] * PIECES, "cd": [None] * PIECES, "cu": [None] * PIECES}

        def pass_on(index, p, device, name, where):
            sib[level, half, index, piece(p)] = kept(level, half, index, p).astype(BF)
            todo[name][p] = send(
                sib.at[level, half, index, piece(p)], land.at[level, half, where, piece(p)], device
            )

        pairs[0].wait_recv()
        for p in range(middle):
            pass_on(0, p, to_down, "b", 0)
            pass_on(0, p + middle, to_up, "b", 0)
        pairs[1].wait_recv()
        for p in range(middle, PIECES):
            pass_on(1, p, to_down, "cd", 1)
        pairs[2].wait_recv()
        for p in range(middle):
            pass_on(2, p, to_up, "cu", 2)
        pairs[3].wait_recv()
        return todo

    def scatter_middle(level, half, todo):
        middle = PIECES // 2
        for step in range(middle):
            for p, index, device, name in (
                (step, 1, to_down, "cd"), (step + middle, 2, to_up, "cu"),
            ):
                todo["b"][p].wait_recv()
                total = kept(level, half, index, p) + land[level, half, 0, piece(p)].astype(F32)
                sib[level, half, index, piece(p)] = total.astype(BF)
                todo[name][p] = send(
                    sib.at[level, half, index, piece(p)], land.at[level, half, index, piece(p)], device
                )

    def scatter_end(level, half, todo, use):
        middle = PIECES // 2
        for step in range(middle):
            for p in (step, step + middle):
                todo["cd"][p].wait_recv()
                todo["cu"][p].wait_recv()
                total = kept(level, half, 3, p)
                total = total + land[level, half, 1, piece(p)].astype(F32)
                use(p, total + land[level, half, 2, piece(p)].astype(F32))

    def hold(p, total):
        held[piece(p)] = total

    parts = gather_start(0)
    table_copy = send(wanted, table_in, to_high)
    pool_load.wait()
    zbuf[pl.ds(z * SLOTS, SLOTS)] = pool_in[...].astype(BF)
    mine = zbuf.at[pl.ds(z * SLOTS, SLOTS)]
    state_copies = [send(mine, mine, device) for device in to_z]
    for level in range(L):
        small_weights(level)
    table_copy.wait_recv()
    table_load = load(table_in, table)
    table_load.wait()
    table_waits = [table_load]

    def states_across():
        for copy in state_copies:
            copy.wait_recv()
        crossing = []
        for entry in range(2 * L):
            asked = table[entry, 0]
            xsend[entry] = zbuf[(asked // (2 * SLOTS)) * SLOTS + asked % SLOTS]
            crossing.append(send(xsend.at[entry], xland.at[entry], to_high))
        return crossing

    for level in range(L):
        if level:
            parts = gather_start(level)
        parts["own"].wait_recv()
        for copy in weight_loads[level]:
            copy.wait()
        project_chunk(level, y)
        gather_near(level, parts)
        parts["down"].wait_recv()
        project_chunk(level, down)
        gather_far(level, parts)
        parts["up"].wait_recv()
        project_chunk(level, up)
        parts["far1"].wait_recv()
        parts["far2"].wait_recv()
        project_chunk(level, far)
        mix_blocks(level, x)
        if level == 0:
            crossing = states_across()
        gather_rest(level, parts)
        if level == 0:
            for copy in crossing:
                copy.wait_recv()
        mix_states(level, x)
        out_loads[level].wait()
        near = scatter_start(level, 0)
        parts["across"].wait_recv()
        for name in ("p3s", "m3s", "x2s"):
            parts[name].wait_recv()
        project_request(level, other)
        mix_blocks(level, other)
        scatter_middle(level, 0, near)
        mix_states(level, other)
        away = scatter_start(level, 1)
        scatter_end(level, 0, near, hold)
        scatter_middle(level, 1, away)
        last = [None] * PIECES

        def cross(p, total):
            sib[level, 1, 3, piece(p)] = total.astype(BF)
            last[p] = send(sib.at[level, 1, 3, piece(p)], last_land.at[level, piece(p)], to_x)

        scatter_end(level, 1, away, cross)
        for p in (0, 2, 1, 3):
            last[p].wait_recv()
            total = held[piece(p)] + last_land[level, piece(p)].astype(F32)
            current[piece(p)] = (current[piece(p)].astype(F32) + total).astype(BF)
    out_rows[...] = current[...]
    for copy in copies:
        copy.wait_send()


def run_layers(
    tokens, in_gain, w_query, w_key, w_value, w_gate, w_beta, w_decay,
    conv_query, conv_key, conv_value, a_log, dt_bias, out_gain, w_out,
    pool, owner, slot, lengths,
):
    wanted = (owner * SLOTS + slot).reshape(2 * L, 1)
    wanted = jnp.broadcast_to(jnp.pad(wanted, ((0, 8 - 2 * L), (0, 0))), (8, 128))
    vmem = pl.BlockSpec(memory_space=pltpu.VMEM)
    smem = pl.BlockSpec(memory_space=pltpu.SMEM)
    hbm = pl.BlockSpec(memory_space=pl.ANY)
    requests = lengths.shape[0]
    scratch = pltpu.VMEM
    return pl.pallas_call(
        layers_kernel,
        name="layers",
        in_specs=[
            vmem, vmem, hbm, hbm, hbm, hbm, vmem, vmem, vmem, vmem, vmem, smem, smem, vmem,
            hbm, hbm, smem, smem, smem, vmem,
        ],
        out_specs=[vmem, vmem],
        out_shape=[
            jax.ShapeDtypeStruct((ROWS, D), BF),
            jax.ShapeDtypeStruct((requests, L, HEADS, DK, DV), F32),
        ],
        scratch_shapes=[
            scratch((L, D, WIDE + 128), BF),
            scratch((L, HEADS * DV, D), BF),
            scratch((L, 16, ROWS, D), BF),
            scratch((2, PAD + SUF, DK), F32),
            scratch((2, PAD + SUF, DK), F32),
            scratch((2, PAD + SUF, HEADS * DV), F32),
            scratch((2, SUF, HEADS * DV), F32),
            scratch((2, SUF, 128), F32),
            scratch((BLOCKS, HEADS, 2 * CHUNK, DK), BF),
            scratch((BLOCKS, HEADS, 2 * CHUNK, DV), F32),
            scratch((BLOCKS, HEADS, 8, DV), F32),
            scratch((SUF, HEADS * DV), BF),
            scratch((L, 2, 4, 2 * ROWS, D), BF),
            scratch((L, 2, 4, ROWS, D), BF),
            scratch((L, 2, 3, ROWS, D), BF),
            scratch((L, ROWS, D), BF),
            scratch((ROWS, D), F32),
            scratch((ROWS, D), BF),
            scratch((SLOTS, HEADS, DK, DV), F32),
            scratch((4 * SLOTS, HEADS, DK, DV), BF),
            scratch((2 * L, HEADS, DK, DV), BF),
            scratch((2 * L, HEADS, DK, DV), BF),
            scratch((8, 128), jnp.int32),
            pltpu.SMEM((8, 128), jnp.int32),
            pltpu.SemaphoreType.DMA((SEMS,)),
            pltpu.SemaphoreType.DMA((SEMS,)),
            pltpu.SemaphoreType.DMA((16,)),
        ],
        compiler_params=pltpu.CompilerParams(
            collective_id=0, has_side_effects=True, vmem_limit_bytes=60 * 1024 * 1024
        ),
    )(
        tokens, in_gain, w_query, w_key, w_value, w_gate,
        w_beta.transpose(0, 2, 1), w_decay.transpose(0, 2, 1),
        conv_query, conv_key, conv_value, a_log, dt_bias, out_gain, w_out,
        pool, owner, slot, lengths, wanted,
    )


def solution(mesh):
    heads = P(None, None, "head")
    in_specs = (
        P(("req", "head"), None), P(), heads, heads, heads, heads, heads, heads,
        heads, heads, heads, P(None, "head"), P(None, "head"), P(),
        P(None, "head", None), P("req", "head", None, None),
        P("req", None), P("req", None), P("req"),
    )
    out_specs = (P(("req", "head"), None), P("req", None, "head", None, None))

    def on_device(*arrays):
        return tuple(run_layers(*arrays))

    return jax.shard_map(
        on_device, mesh=mesh, in_specs=in_specs, out_specs=out_specs, check_vma=False
    )
```

```python
import jax
import jax.numpy as jnp
from jax import lax
from jax.experimental import pallas as pl
from jax.experimental.pallas import tpu as pltpu
from jax.sharding import PartitionSpec as P

DK = 128
DV = 128
L = 2
SLOTS = 4
SUF = 512
CONV = 4
HEADS = 2
CHUNK = 128
BLOCKS = SUF // CHUNK
PAD = 8
EPS = 1e-06
BF = jnp.bfloat16
F32 = jnp.float32
D = 2048
ROWS = 64
PIECE = 16
PIECES = ROWS // PIECE
ORDER = (0, 2, 1, 3)
WIDE = 2 * DK + 2 * HEADS * DV
SEMS = 176


def silu(v):
    return v / (1.0 + jnp.exp(-v))


def conv_block(ref, row, width, taps):
    window = ref[pl.ds(row, CHUNK + PAD), 0:width]
    total = None
    for tap in range(CONV):
        first = PAD - (CONV - 1) + tap
        term = window[first : first + CHUNK] * taps[tap : tap + 1]
        total = term if total is None else total + term
    return silu(total)


def unit_rows(vectors):
    return vectors * lax.rsqrt(jnp.sum(vectors * vectors, -1, keepdims=True) + EPS)


def mm(a, b):
    return jnp.dot(a.astype(BF), b.astype(BF), preferred_element_type=F32)


def nt(a, b):
    return lax.dot_general(
        a.astype(BF), b.astype(BF), (((1,), (1,)), ((), ())), preferred_element_type=F32
    )


def lower_inverses(stricts, rows, cols):
    size = 16
    near = rows // size == cols // size
    eye = jnp.where(rows == cols, 1.0, 0.0)
    diags = [jnp.where(near, -strict, 0.0) for strict in stricts]
    inverses = [eye + diag for diag in diags]
    powers = [mm(diag, diag) for diag in diags]
    for _ in range(2):
        both = [
            mm(jnp.concatenate([power, inverse], 0), power)
            for power, inverse in zip(powers, inverses)
        ]
        inverses = [inverse + pair[CHUNK:] for inverse, pair in zip(inverses, both)]
        powers = [pair[:CHUNK] for pair in both]
    inverses = [inverse + mm(inverse, power) for inverse, power in zip(inverses, powers)]
    while size < CHUNK:
        joined = (rows // (2 * size) == cols // (2 * size)) & (rows // size > cols // size)
        halves = [
            mm(jnp.where(joined, strict, 0.0), inverse)
            for strict, inverse in zip(stricts, inverses)
        ]
        inverses = [inverse - mm(inverse, half) for inverse, half in zip(inverses, halves)]
        size *= 2
    return inverses


def gate_rows(raw, a_log, dt_bias, valid):
    rows = []
    for head in range(HEADS):
        rows.append(jnp.where(valid, 1.0 / (1.0 + jnp.exp(-raw[head : head + 1])), 0.0))
    for head in range(HEADS):
        shifted = raw[HEADS + head : HEADS + head + 1] + dt_bias[head]
        soft = jnp.maximum(shifted, 0.0) + jnp.log1p(jnp.exp(-jnp.abs(shifted)))
        rate = jnp.exp(jnp.full((1, CHUNK), a_log[head], F32))
        rows.append(jnp.where(valid, -rate * soft, 0.0))
    rows.append(jnp.zeros((8 - 2 * HEADS, CHUNK), F32))
    return jnp.concatenate(rows, 0)


def block_terms(blocks, q_ref, k_ref, v_ref, raws, taps, a_log, dt_bias, length, move_ref, add_ref, tail_ref):
    rows = lax.broadcasted_iota(jnp.int32, (CHUNK, CHUNK), 0)
    cols = lax.broadcasted_iota(jnp.int32, (CHUNK, CHUNK), 1)
    lane = lax.broadcasted_iota(jnp.int32, (1, CHUNK), 1)
    upper = jnp.where(rows <= cols, 1.0, 0.0)
    gates = [
        gate_rows(raw, a_log, dt_bias, block * CHUNK + lane < length)
        for block, raw in zip(blocks, raws)
    ]
    sums = jnp.dot(
        jnp.concatenate(gates, 0), upper, precision=lax.Precision.HIGHEST, preferred_element_type=F32
    )
    sums = [sums[8 * index : 8 * index + 8] for index in range(len(blocks))]
    columns = [jnp.concatenate([gate, total], 0).T for gate, total in zip(gates, sums)]
    keys = [unit_rows(conv_block(k_ref, block * CHUNK, DK, taps[1])) for block in blocks]
    queries = [
        unit_rows(conv_block(q_ref, block * CHUNK, DK, taps[0])) * DK ** (-0.5) for block in blocks
    ]
    dots = [nt(jnp.concatenate([key, query], 0), key) for key, query in zip(keys, queries)]
    units = [(index, head) for index in range(len(blocks)) for head in range(HEADS)]
    stricts, decays = [], []
    for index, head in units:
        cumul = columns[index][:, 8 + HEADS + head : 9 + HEADS + head]
        cumul_row = sums[index][HEADS + head : HEADS + head + 1]
        decay = jnp.where(rows >= cols, jnp.exp(jnp.minimum(cumul - cumul_row, 0.0)), 0.0)
        beta = columns[index][:, head : head + 1]
        stricts.append(jnp.where(rows > cols, dots[index][:CHUNK] * decay * beta, 0.0))
        decays.append(decay)
    inverses = lower_inverses(stricts, rows, cols)
    values = [conv_block(v_ref, block * CHUNK, HEADS * DV, taps[2]) for block in blocks]
    solved = []
    for (index, head), inverse in zip(units, inverses):
        beta = columns[index][:, head : head + 1]
        grown = jnp.exp(columns[index][:, 8 + HEADS + head : 9 + HEADS + head])
        right = jnp.concatenate(
            [values[index][:, head * DV : (head + 1) * DV] * beta, keys[index] * (beta * grown)], 1
        )
        solved.append(mm(inverse, right))
    for (index, head), decay, solution_now in zip(units, decays, solved):
        cumul = columns[index][:, 8 + HEADS + head : 9 + HEADS + head]
        last = cumul[CHUNK - 1 :]
        key_tail = keys[index] * jnp.exp(last - cumul)
        mixing = dots[index][CHUNK:] * decay
        both = mm(jnp.concatenate([key_tail.T, mixing], 0), solution_now)
        move = jnp.concatenate(
            [-both[:DK, DV:], queries[index] * jnp.exp(cumul) - both[DK:, DV:]], 0
        )
        move_ref[blocks[index], head] = move.astype(BF)
        add_ref[blocks[index], head] = both[:, :DV]
        tail_ref[blocks[index], head] = jnp.broadcast_to(jnp.exp(last), (8, DV))


def run_states(start, move_ref, add_ref, tail_ref, z_ref, gain, length, store):
    states = [start[head] for head in range(HEADS)]
    for block in range(BLOCKS):
        place = block * CHUNK + lax.broadcasted_iota(jnp.int32, (CHUNK, 1), 0)
        valid = (place < length).astype(F32)
        results = [
            mm(move_ref[block, head], states[head]) + add_ref[block, head] for head in range(HEADS)
        ]
        for head in range(HEADS):
            states[head] = tail_ref[block, head][0:1] * states[head] + results[head][:DK]
            out = results[head][DK:]
            scale = lax.rsqrt(jnp.mean(out * out, -1, keepdims=True) + EPS)
            gate = z_ref[pl.ds(block * CHUNK, CHUNK), head * DV : (head + 1) * DV]
            store(block, head, (out * scale * gain * silu(gate) * valid).astype(BF))
    return states


def spot(x, y, core):
    return x * 8 + y * 2 + core


def piece(index):
    return pl.ds(index * PIECE, PIECE)


def layers_kernel(
    tokens, in_gain_hbm, w_query, w_key, w_value, w_gate, w_beta_hbm, w_decay_hbm,
    conv_query_hbm, conv_key_hbm, conv_value_hbm, a_log_hbm, dt_bias_hbm, out_gain_hbm, w_out,
    pool, owner_hbm, slot_hbm, lengths_hbm,
    out_rows, final_hbm,
    weights, outs, buf, q_ref, k_ref, v_ref, z_ref, raw_ref, move_ref, add_ref, tail_ref,
    mixed, stage, sib, land, current, pool_in, zbuf, xsend, xland,
    wanted, table_in, table, in_gain, w_beta, w_decay, conv_query, conv_key, conv_value, out_gain,
    a_log, dt_bias, owner, slot, lengths, final, send_sems, recv_sems, local_sems,
):
    me = lax.axis_index("head")
    group = lax.axis_index("req")
    x, y, core = me // 8, (me // 2) % 4, me % 2
    z, high = group // 2, group % 2
    other, up, down, far = 1 - x, (y + 1) % 4, (y + 3) % 4, (y + 2) % 4
    middle = PIECES // 2

    to_x = {"head": spot(other, y, core)}
    to_up, to_down = {"head": spot(x, up, core)}, {"head": spot(x, down, core)}
    sibling = {"head": spot(x, y, 1 - core)}
    to_high = {"req": z * 2 + 1 - high}
    to_z = [{"req": ((z + step) % 4) * 2 + high} for step in (1, 3, 2)]

    count = [0]

    def remote(source, target, device):
        index = count[0]
        count[0] += 1
        return pltpu.make_async_remote_copy(
            src_ref=source,
            dst_ref=target,
            send_sem=send_sems.at[index],
            recv_sem=recv_sems.at[index],
            device_id=device,
            device_id_type=pl.DeviceIdType.MESH,
        )

    def same(ref, device):
        return remote(ref, ref, device)

    class Moves:
        def __init__(self, level, request):
            def block(b):
                return buf.at[level, spot(request, b, core)]

            def part(b, p):
                return buf.at[level, spot(request, b, core), piece(p)]

            halves = [pl.ds(0, ROWS // 2), pl.ds(ROWS // 2, ROWS // 2)]
            self.across = []
            if level == 0:
                self.across = [same(current.at[request, piece(p)], to_x) for p in range(PIECES)]
            self.ups = [same(part(y, p), to_up) for p in range(PIECES)]
            self.downs = [same(part(y, p), to_down) for p in range(PIECES)]
            self.fars = [
                same(part(down, p), to_up) if p < middle else same(part(up, p), to_down)
                for p in range(PIECES)
            ]
            self.own_core = same(block(y), sibling)
            self.down_core = same(block(down), sibling)
            self.up_core = same(block(up), sibling)
            self.far_core = [
                same(buf.at[level, spot(request, far, core), rows], sibling) for rows in halves
            ]
            here = (level, request)
            theirs = pl.ds(pl.multiple_of((1 - core) * ROWS, ROWS), ROWS)
            self.pairs = [
                remote(stage.at[(*here, index, theirs)], sib.at[(*here, index)], sibling)
                for index in range(4)
            ]

            def part_sum(index, p, device):
                return remote(
                    sib.at[(*here, index, piece(p))], land.at[(*here, index, piece(p))], device
                )

            self.far_sums = [
                part_sum(0, p, to_down if p < middle else to_up) for p in range(PIECES)
            ]
            self.down_sums = [part_sum(1, p, to_down) for p in range(PIECES)]
            self.up_sums = [part_sum(2, p, to_up) for p in range(PIECES)]
            self.cross_sums = [part_sum(3, p, to_x) for p in range(PIECES)]

        def always(self):
            return (
                self.ups + self.downs + self.fars
                + [self.own_core, self.down_core, self.up_core] + self.far_core
                + self.pairs + self.far_sums + self.down_sums + self.up_sums
            )

    moves = [[Moves(level, request) for request in range(2)] for level in range(L)]

    loads, stores = [], []

    def load(source, target):
        copy = pltpu.make_async_copy(source, target, local_sems.at[len(loads)])
        copy.start()
        loads.append(copy)
        return copy

    open_loads = [load(tokens, current.at[x]), load(in_gain_hbm, in_gain)]
    pool_loads = [load(owner_hbm, owner), load(slot_hbm, slot), load(pool, pool_in)]
    small_loads = [load(w_beta_hbm, w_beta), load(w_decay_hbm, w_decay)]
    mix_loads = [
        load(source, target)
        for source, target in (
            (conv_query_hbm, conv_query), (conv_key_hbm, conv_key), (conv_value_hbm, conv_value),
            (a_log_hbm, a_log), (dt_bias_hbm, dt_bias), (out_gain_hbm, out_gain),
            (lengths_hbm, lengths),
        )
    ]
    weight_loads, out_loads = [], []
    for level in range(L):
        first = 0
        mine = []
        for source, width in (
            (w_query, DK), (w_key, DK), (w_value, HEADS * DV), (w_gate, HEADS * DV),
        ):
            mine.append(load(source.at[level], weights.at[level, :, pl.ds(first, width)]))
            first += width
        weight_loads.append(mine)
        out_loads.append(load(w_out.at[level], outs.at[level]))

    barrier = pltpu.get_barrier_semaphore()
    partners = [to_x, to_up, to_down, sibling, to_high] + to_z
    for partner in partners:
        pl.semaphore_signal(
            barrier, inc=1, device_id=partner, device_id_type=pl.DeviceIdType.MESH
        )
    pl.semaphore_wait(barrier, len(partners))
    for copy in open_loads:
        copy.wait()

    def spread_piece(level, request, p):
        floats = current[request, piece(p)].astype(F32)
        scale = lax.rsqrt(jnp.mean(floats * floats, -1, keepdims=True) + EPS)
        normed = (floats * scale * in_gain[level : level + 1]).astype(BF)
        buf[level, spot(request, y, core), piece(p)] = normed
        moves[level][request].ups[p].start()
        moves[level][request].downs[p].start()

    def open_request(request):
        move = moves[0][request]
        for p in ORDER:

            @pl.when(x != request)
            def _():
                move.across[p].wait_recv()

            spread_piece(0, request, p)
        move.own_core.start()

    def gather_near(level, request):
        move = moves[level][request]
        for p in ORDER:
            move.ups[p].wait_recv()
            if p < middle:
                move.fars[p].start()
            move.downs[p].wait_recv()
            if p >= middle:
                move.fars[p].start()
        move.down_core.start()
        move.up_core.start()

    def gather_far(level, request):
        move = moves[level][request]
        for first in (0, middle):
            for p in range(first, first + middle):
                move.fars[p].wait_recv()
            move.far_core[first // middle].start()

    def small_weights(level):
        rows = jnp.concatenate(
            [
                w_beta[level].astype(F32),
                w_decay[level].astype(F32),
                jnp.zeros((128 - 2 * HEADS, D), F32),
            ],
            0,
        )
        weights[level, :, WIDE:] = rows.T.astype(BF)

    def keep(request, result, row, rows):
        place = pl.ds(row + PAD, rows)
        q_ref[request, place] = result[:, 0:DK]
        k_ref[request, place] = result[:, DK : 2 * DK]
        v_ref[request, place] = result[:, 2 * DK : 2 * DK + HEADS * DV]
        z_ref[request, pl.ds(row, rows)] = result[:, 2 * DK + HEADS * DV : WIDE]
        raw_ref[request, pl.ds(row, rows)] = result[:, WIDE:]

    def project_chunk(level, request, b):
        rows = buf[level, pl.ds(spot(request, b, 0), 2)].reshape(CHUNK, D)
        result = jnp.dot(rows, weights[level], preferred_element_type=F32)
        keep(request, result, pl.multiple_of(b * CHUNK, CHUNK), CHUNK)

    def project_request(level, request):
        rows = buf[level, pl.ds(request * 8, 8)].reshape(SUF, D)
        result = jnp.dot(rows, weights[level], preferred_element_type=F32)
        keep(request, result, 0, SUF)

    def mix_blocks(level, request):
        blocks = list(range(BLOCKS))
        raws = [
            raw_ref[request, pl.ds(block * CHUNK, CHUNK)].T[0 : 2 * HEADS] for block in blocks
        ]
        block_terms(
            blocks, q_ref.at[request], k_ref.at[request], v_ref.at[request], raws,
            (conv_query[level], conv_key[level], conv_value[level]),
            [a_log[level, head] for head in range(HEADS)],
            [dt_bias[level, head] for head in range(HEADS)],
            lengths[request], move_ref, add_ref, tail_ref,
        )

    def mix_states(level, request):
        holder = owner[request, level]
        near = zbuf[(holder // 2) * SLOTS + slot[request, level]]
        start = jnp.where(holder % 2 == high, near, xland[request * L + level]).astype(F32)

        def store(block, head, rows):
            mixed[pl.ds(block * CHUNK, CHUNK), head * DV : (head + 1) * DV] = rows

        states = run_states(
            start, move_ref, add_ref, tail_ref, z_ref.at[request], out_gain[level : level + 1],
            lengths[request], store,
        )
        for head in range(HEADS):
            final[request, level, head] = states[head]
        stores.append(load(final.at[request, level], final_hbm.at[request, level]))

    def kept(level, request, index, p):
        row = pl.multiple_of(core * ROWS + p * PIECE, PIECE)
        mine = stage[level, request, index, pl.ds(row, PIECE)].astype(F32)
        return mine + sib[level, request, index, piece(p)].astype(F32)

    def scatter_start(level, request):
        move = moves[level][request]

        def term(index, b):
            rows = mixed[pl.ds(pl.multiple_of(b * CHUNK, CHUNK), CHUNK)]
            stage[level, request, index] = jnp.dot(
                rows, outs[level], preferred_element_type=F32
            ).astype(BF)
            move.pairs[index].start()

        def pass_on(index, p, copy):
            sib[level, request, index, piece(p)] = kept(level, request, index, p).astype(BF)
            copy.start()

        term(0, far)
        term(1, down)
        term(2, up)
        move.pairs[0].wait_recv()
        for p in range(middle):
            pass_on(0, p, move.far_sums[p])
            pass_on(0, p + middle, move.far_sums[p + middle])
        term(3, y)
        move.pairs[1].wait_recv()
        move.pairs[2].wait_recv()
        for p in range(middle):
            pass_on(1, p + middle, move.down_sums[p + middle])
            pass_on(2, p, move.up_sums[p])
        move.pairs[3].wait_recv()

    def scatter_middle(level, request):
        move = moves[level][request]
        for step in range(middle):
            for p, index, sums in (
                (step, 1, move.down_sums), (step + middle, 2, move.up_sums),
            ):
                move.far_sums[p].wait_recv()
                total = kept(level, request, index, p)
                total = total + land[level, request, 0, piece(p)].astype(F32)
                sib[level, request, index, piece(p)] = total.astype(BF)
                sums[p].start()

    def scatter_end(level, request):
        move = moves[level][request]
        for p in ORDER:
            move.down_sums[p].wait_recv()
            move.up_sums[p].wait_recv()
            total = kept(level, request, 3, p)
            total = total + land[level, request, 1, piece(p)].astype(F32)
            total = total + land[level, request, 2, piece(p)].astype(F32)
            sib[level, request, 3, piece(p)] = total.astype(BF)
            if level + 1 < L:
                move.cross_sums[p].start()
            else:

                @pl.when(x != request)
                def _():
                    move.cross_sums[p].start()

    def add_piece(level, request, p):
        moves[level][request].cross_sums[p].wait_recv()
        total = sib[level, request, 3, piece(p)].astype(F32)
        total = total + land[level, request, 3, piece(p)].astype(F32)
        old = current[request, piece(p)].astype(F32)
        current[request, piece(p)] = (old + total).astype(BF)

    def next_rows(level, request):
        if level + 1 < L:

            @pl.when(x == request)
            def _():
                for copy in moves[level][request].across:
                    copy.wait_send()

            for p in ORDER:
                add_piece(level, request, p)
                spread_piece(level + 1, request, p)
            moves[level + 1][request].own_core.start()
        else:

            @pl.when(x == request)
            def _():
                for p in ORDER:
                    add_piece(level, request, p)

    for request in range(2):

        @pl.when(x == request)
        def _():
            for p in ORDER:
                moves[0][request].across[p].start()

    open_request(0)

    for copy in pool_loads:
        copy.wait()
    entry_rows = lax.broadcasted_iota(jnp.int32, (8, 128), 0)
    asks = jnp.zeros((8, 128), jnp.int32)
    for entry in range(2 * L):
        row = owner[entry // L, entry % L] * SLOTS + slot[entry // L, entry % L]
        asks = jnp.where(entry_rows == entry, row, asks)
    wanted[...] = asks
    table_copy = remote(wanted, table_in, to_high)
    table_copy.start()
    zbuf[pl.ds(z * SLOTS, SLOTS)] = pool_in[...].astype(BF)
    state_copies = [same(zbuf.at[pl.ds(z * SLOTS, SLOTS)], device) for device in to_z]
    for copy in state_copies[:2]:
        copy.start()
    for ref in (q_ref, k_ref, v_ref):
        ref[:, 0:PAD] = jnp.zeros((2, PAD, ref.shape[2]), F32)
    for copy in small_loads:
        copy.wait()
    small_weights(0)
    for copy in mix_loads:
        copy.wait()
    crossing = [remote(xsend.at[entry], xland.at[entry], to_high) for entry in range(2 * L)]

    def states_across():
        table_copy.wait_recv()
        table_load = load(table_in, table)
        for copy in state_copies:
            copy.wait_recv()
        table_load.wait()
        for entry in range(2 * L):
            asked = table[entry, 0]
            xsend[entry] = zbuf[(asked // (2 * SLOTS)) * SLOTS + asked % SLOTS]
            crossing[entry].start()

    for level in range(L):
        if level:
            scatter_end(0, 0)
            scatter_middle(0, 1)
            next_rows(0, 0)
            scatter_end(0, 1)
        for copy in weight_loads[level]:
            copy.wait()
        move = moves[level][0]
        move.own_core.wait_recv()
        project_chunk(level, 0, y)
        gather_near(level, 0)
        if level:
            next_rows(0, 1)
        else:
            state_copies[2].start()
            open_request(1)
        move.down_core.wait_recv()
        project_chunk(level, 0, down)
        gather_far(level, 0)
        move.up_core.wait_recv()
        project_chunk(level, 0, up)
        for copy in move.far_core:
            copy.wait_recv()
        project_chunk(level, 0, far)
        gather_near(level, 1)
        if level == 0:
            states_across()
        mix_blocks(level, 0)
        gather_far(level, 1)
        if level == 0:
            for copy in crossing:
                copy.wait_recv()
            small_weights(1)
        mix_states(level, 0)
        out_loads[level].wait()
        scatter_start(level, 0)
        move = moves[level][1]
        for copy in [move.own_core, move.down_core, move.up_core] + move.far_core:
            copy.wait_recv()
        project_request(level, 1)
        mix_blocks(level, 1)
        scatter_middle(level, 0)
        mix_states(level, 1)
        scatter_start(level, 1)
    scatter_end(1, 0)
    scatter_middle(1, 1)
    next_rows(1, 0)
    scatter_end(1, 1)
    next_rows(1, 1)
    stores.append(load(current.at[x], out_rows))
    for copy in stores:
        copy.wait()
    for copy in [table_copy] + state_copies + crossing:
        copy.wait_send()
    for level in range(L):
        for request in range(2):
            move = moves[level][request]
            for copy in move.always():
                copy.wait_send()

            if level == 0:
                for copy in move.cross_sums:
                    copy.wait_send()
            else:

                @pl.when(x != request)
                def _():
                    for copy in move.cross_sums:
                        copy.wait_send()


def run_layers(
    tokens, in_gain, w_query, w_key, w_value, w_gate, w_beta, w_decay,
    conv_query, conv_key, conv_value, a_log, dt_bias, out_gain, w_out,
    pool, owner, slot, lengths,
):
    requests = lengths.shape[0]
    scratch = pltpu.VMEM
    return pl.pallas_call(
        layers_kernel,
        name="layers",
        in_specs=[pl.BlockSpec(memory_space=pl.ANY)] * 19,
        out_specs=[pl.BlockSpec(memory_space=pl.ANY)] * 2,
        out_shape=[
            jax.ShapeDtypeStruct((ROWS, D), BF),
            jax.ShapeDtypeStruct((requests, L, HEADS, DK, DV), F32),
        ],
        scratch_shapes=[
            scratch((L, D, WIDE + 128), BF),
            scratch((L, HEADS * DV, D), BF),
            scratch((L, 16, ROWS, D), BF),
            scratch((2, PAD + SUF, DK), F32),
            scratch((2, PAD + SUF, DK), F32),
            scratch((2, PAD + SUF, HEADS * DV), F32),
            scratch((2, SUF, HEADS * DV), F32),
            scratch((2, SUF, 128), F32),
            scratch((BLOCKS, HEADS, 2 * CHUNK, DK), BF),
            scratch((BLOCKS, HEADS, 2 * CHUNK, DV), F32),
            scratch((BLOCKS, HEADS, 8, DV), F32),
            scratch((SUF, HEADS * DV), BF),
            scratch((L, 2, 4, 2 * ROWS, D), BF),
            scratch((L, 2, 4, ROWS, D), BF),
            scratch((L, 2, 4, ROWS, D), BF),
            scratch((2, ROWS, D), BF),
            scratch((SLOTS, HEADS, DK, DV), F32),
            scratch((4 * SLOTS, HEADS, DK, DV), BF),
            scratch((2 * L, HEADS, DK, DV), BF),
            scratch((2 * L, HEADS, DK, DV), BF),
            scratch((8, 128), jnp.int32),
            scratch((8, 128), jnp.int32),
            pltpu.SMEM((8, 128), jnp.int32),
            scratch((L, D), F32),
            scratch((L, HEADS, D), BF),
            scratch((L, HEADS, D), BF),
            scratch((L, CONV, DK), F32),
            scratch((L, CONV, DK), F32),
            scratch((L, CONV, HEADS * DV), F32),
            scratch((L, DV), F32),
            pltpu.SMEM((L, HEADS), F32),
            pltpu.SMEM((L, HEADS), F32),
            pltpu.SMEM((requests, L), jnp.int32),
            pltpu.SMEM((requests, L), jnp.int32),
            pltpu.SMEM((requests,), jnp.int32),
            scratch((requests, L, HEADS, DK, DV), F32),
            pltpu.SemaphoreType.DMA((SEMS,)),
            pltpu.SemaphoreType.DMA((SEMS,)),
            pltpu.SemaphoreType.DMA((40,)),
        ],
        compiler_params=pltpu.CompilerParams(
            collective_id=0, has_side_effects=True, vmem_limit_bytes=60 * 1024 * 1024
        ),
    )(
        tokens, in_gain, w_query, w_key, w_value, w_gate,
        w_beta.transpose(0, 2, 1), w_decay.transpose(0, 2, 1),
        conv_query, conv_key, conv_value, a_log, dt_bias, out_gain, w_out,
        pool, owner, slot, lengths,
    )


def solution(mesh):
    heads = P(None, None, "head")
    in_specs = (
        P(("req", "head"), None), P(), heads, heads, heads, heads, heads, heads,
        heads, heads, heads, P(None, "head"), P(None, "head"), P(),
        P(None, "head", None), P("req", "head", None, None),
        P("req", None), P("req", None), P("req"),
    )
    out_specs = (P(("req", "head"), None), P("req", None, "head", None, None))

    def on_device(*arrays):
        return tuple(run_layers(*arrays))

    return jax.shard_map(
        on_device, mesh=mesh, in_specs=in_specs, out_specs=out_specs, check_vma=False
    )
```

```python
import jax
import jax.numpy as jnp
from jax import lax
from jax.experimental import pallas as pl
from jax.experimental.pallas import tpu as pltpu
from jax.sharding import PartitionSpec as P

DK = 128
DV = 128
L = 2
SLOTS = 4
SUF = 512
CONV = 4
HEADS = 2
CHUNK = 128
BLOCKS = SUF // CHUNK
PAD = 8
EPS = 1e-06
BF = jnp.bfloat16
F32 = jnp.float32
D = 2048
ROWS = 64
PIECE = 16
PIECES = ROWS // PIECE
ORDER = (0, 2, 1, 3)
WIDE = 2 * DK + 2 * HEADS * DV
SEMS = 176


def silu(v):
    return v / (1.0 + jnp.exp(-v))


def conv_block(ref, row, width, taps):
    window = ref[pl.ds(row, CHUNK + PAD), 0:width]
    total = None
    for tap in range(CONV):
        first = PAD - (CONV - 1) + tap
        term = window[first : first + CHUNK] * taps[tap : tap + 1]
        total = term if total is None else total + term
    return silu(total)


def unit_rows(vectors):
    return vectors * lax.rsqrt(jnp.sum(vectors * vectors, -1, keepdims=True) + EPS)


def mm(a, b):
    return jnp.dot(a.astype(BF), b.astype(BF), preferred_element_type=F32)


def nt(a, b):
    return lax.dot_general(
        a.astype(BF), b.astype(BF), (((1,), (1,)), ((), ())), preferred_element_type=F32
    )


def lower_inverses(stricts, rows, cols):
    size = 16
    near = rows // size == cols // size
    eye = jnp.where(rows == cols, 1.0, 0.0)
    diags = [jnp.where(near, -strict, 0.0) for strict in stricts]
    inverses = [eye + diag for diag in diags]
    powers = [mm(diag, diag) for diag in diags]
    for _ in range(2):
        both = [
            mm(jnp.concatenate([power, inverse], 0), power)
            for power, inverse in zip(powers, inverses)
        ]
        inverses = [inverse + pair[CHUNK:] for inverse, pair in zip(inverses, both)]
        powers = [pair[:CHUNK] for pair in both]
    inverses = [inverse + mm(inverse, power) for inverse, power in zip(inverses, powers)]
    while size < CHUNK:
        joined = (rows // (2 * size) == cols // (2 * size)) & (rows // size > cols // size)
        halves = [
            mm(jnp.where(joined, strict, 0.0), inverse)
            for strict, inverse in zip(stricts, inverses)
        ]
        inverses = [inverse - mm(inverse, half) for inverse, half in zip(inverses, halves)]
        size *= 2
    return inverses


def gate_rows(raw, a_log, dt_bias, valid):
    rows = []
    for head in range(HEADS):
        rows.append(jnp.where(valid, 1.0 / (1.0 + jnp.exp(-raw[head : head + 1])), 0.0))
    for head in range(HEADS):
        shifted = raw[HEADS + head : HEADS + head + 1] + dt_bias[head]
        soft = jnp.maximum(shifted, 0.0) + jnp.log1p(jnp.exp(-jnp.abs(shifted)))
        rate = jnp.exp(jnp.full((1, CHUNK), a_log[head], F32))
        rows.append(jnp.where(valid, -rate * soft, 0.0))
    rows.append(jnp.zeros((8 - 2 * HEADS, CHUNK), F32))
    return jnp.concatenate(rows, 0)


def block_terms(blocks, q_ref, k_ref, v_ref, raws, taps, a_log, dt_bias, length, move_ref, add_ref, tail_ref):
    rows = lax.broadcasted_iota(jnp.int32, (CHUNK, CHUNK), 0)
    cols = lax.broadcasted_iota(jnp.int32, (CHUNK, CHUNK), 1)
    lane = lax.broadcasted_iota(jnp.int32, (1, CHUNK), 1)
    upper = jnp.where(rows <= cols, 1.0, 0.0)
    gates = [
        gate_rows(raw, a_log, dt_bias, block * CHUNK + lane < length)
        for block, raw in zip(blocks, raws)
    ]
    sums = jnp.dot(
        jnp.concatenate(gates, 0), upper, precision=lax.Precision.HIGHEST, preferred_element_type=F32
    )
    sums = [sums[8 * index : 8 * index + 8] for index in range(len(blocks))]
    columns = [jnp.concatenate([gate, total], 0).T for gate, total in zip(gates, sums)]
    keys = [unit_rows(conv_block(k_ref, block * CHUNK, DK, taps[1])) for block in blocks]
    queries = [
        unit_rows(conv_block(q_ref, block * CHUNK, DK, taps[0])) * DK ** (-0.5) for block in blocks
    ]
    dots = [nt(jnp.concatenate([key, query], 0), key) for key, query in zip(keys, queries)]
    units = [(index, head) for index in range(len(blocks)) for head in range(HEADS)]
    stricts, decays = [], []
    for index, head in units:
        cumul = columns[index][:, 8 + HEADS + head : 9 + HEADS + head]
        cumul_row = sums[index][HEADS + head : HEADS + head + 1]
        decay = jnp.where(rows >= cols, jnp.exp(jnp.minimum(cumul - cumul_row, 0.0)), 0.0)
        beta = columns[index][:, head : head + 1]
        stricts.append(jnp.where(rows > cols, dots[index][:CHUNK] * decay * beta, 0.0))
        decays.append(decay)
    inverses = lower_inverses(stricts, rows, cols)
    values = [conv_block(v_ref, block * CHUNK, HEADS * DV, taps[2]) for block in blocks]
    solved = []
    for (index, head), inverse in zip(units, inverses):
        beta = columns[index][:, head : head + 1]
        grown = jnp.exp(columns[index][:, 8 + HEADS + head : 9 + HEADS + head])
        right = jnp.concatenate(
            [values[index][:, head * DV : (head + 1) * DV] * beta, keys[index] * (beta * grown)], 1
        )
        solved.append(mm(inverse, right))
    for (index, head), decay, solution_now in zip(units, decays, solved):
        cumul = columns[index][:, 8 + HEADS + head : 9 + HEADS + head]
        last = cumul[CHUNK - 1 :]
        key_tail = keys[index] * jnp.exp(last - cumul)
        mixing = dots[index][CHUNK:] * decay
        both = mm(jnp.concatenate([key_tail.T, mixing], 0), solution_now)
        move = jnp.concatenate(
            [-both[:DK, DV:], queries[index] * jnp.exp(cumul) - both[DK:, DV:]], 0
        )
        move_ref[blocks[index], head] = move.astype(BF)
        add_ref[blocks[index], head] = both[:, :DV]
        tail_ref[blocks[index], head] = jnp.broadcast_to(jnp.exp(last), (8, DV))


def run_states(start, move_ref, add_ref, tail_ref, z_ref, gain, length, store):
    states = [start[head] for head in range(HEADS)]
    for block in range(BLOCKS):
        place = block * CHUNK + lax.broadcasted_iota(jnp.int32, (CHUNK, 1), 0)
        valid = (place < length).astype(F32)
        results = [
            mm(move_ref[block, head], states[head]) + add_ref[block, head] for head in range(HEADS)
        ]
        for head in range(HEADS):
            states[head] = tail_ref[block, head][0:1] * states[head] + results[head][:DK]
            out = results[head][DK:]
            scale = lax.rsqrt(jnp.mean(out * out, -1, keepdims=True) + EPS)
            gate = z_ref[pl.ds(block * CHUNK, CHUNK), head * DV : (head + 1) * DV]
            store(block, head, (out * scale * gain * silu(gate) * valid).astype(BF))
    return states


def spot(x, y, core):
    return x * 8 + y * 2 + core


def piece(index):
    return pl.ds(index * PIECE, PIECE)


def layers_kernel(
    tokens, in_gain_hbm, w_query, w_key, w_value, w_gate, w_beta_hbm, w_decay_hbm,
    conv_query_hbm, conv_key_hbm, conv_value_hbm, a_log_hbm, dt_bias_hbm, out_gain_hbm, w_out,
    pool, owner_hbm, slot_hbm, lengths_hbm,
    out_rows, final_hbm,
    weights, outs, buf, q_ref, k_ref, v_ref, z_ref, raw_ref, move_ref, add_ref, tail_ref,
    mixed, stage, sib, land, current, pool_in, zbuf, xsend, xland,
    wanted, table_in, table, in_gain, w_beta, w_decay, conv_query, conv_key, conv_value, out_gain,
    a_log, dt_bias, owner, slot, lengths, final, send_sems, recv_sems, local_sems,
):
    me = lax.axis_index("head")
    group = lax.axis_index("req")
    x, y, core = me // 8, (me // 2) % 4, me % 2
    z, high = group // 2, group % 2
    other, up, down, far = 1 - x, (y + 1) % 4, (y + 3) % 4, (y + 2) % 4
    middle = PIECES // 2

    to_x = {"head": spot(other, y, core)}
    to_up, to_down = {"head": spot(x, up, core)}, {"head": spot(x, down, core)}
    sibling = {"head": spot(x, y, 1 - core)}
    to_high = {"req": z * 2 + 1 - high}
    to_z = [{"req": ((z + step) % 4) * 2 + high} for step in (1, 3, 2)]

    count = [0]

    def remote(source, target, device):
        index = count[0]
        count[0] += 1
        return pltpu.make_async_remote_copy(
            src_ref=source,
            dst_ref=target,
            send_sem=send_sems.at[index],
            recv_sem=recv_sems.at[index],
            device_id=device,
            device_id_type=pl.DeviceIdType.MESH,
        )

    def same(ref, device):
        return remote(ref, ref, device)

    class Moves:
        def __init__(self, level, request):
            def block(b):
                return buf.at[level, spot(request, b, core)]

            def part(b, p):
                return buf.at[level, spot(request, b, core), piece(p)]

            halves = [pl.ds(0, ROWS // 2), pl.ds(ROWS // 2, ROWS // 2)]
            self.across = []
            if level == 0:
                self.across = [same(current.at[request, piece(p)], to_x) for p in range(PIECES)]
            self.ups = [same(part(y, p), to_up) for p in range(PIECES)]
            self.downs = [same(part(y, p), to_down) for p in range(PIECES)]
            self.fars = [
                same(part(down, p), to_up) if p < middle else same(part(up, p), to_down)
                for p in range(PIECES)
            ]
            self.own_core = same(block(y), sibling)
            self.down_core = same(block(down), sibling)
            self.up_core = same(block(up), sibling)
            self.far_core = [
                same(buf.at[level, spot(request, far, core), rows], sibling) for rows in halves
            ]
            here = (level, request)
            theirs = pl.ds(pl.multiple_of((1 - core) * ROWS, ROWS), ROWS)
            self.pairs = [
                remote(stage.at[(*here, index, theirs)], sib.at[(*here, index)], sibling)
                for index in range(4)
            ]

            def part_sum(index, p, device):
                return remote(
                    sib.at[(*here, index, piece(p))], land.at[(*here, index, piece(p))], device
                )

            self.far_sums = [
                part_sum(0, p, to_down if p < middle else to_up) for p in range(PIECES)
            ]
            self.down_sums = [part_sum(1, p, to_down) for p in range(PIECES)]
            self.up_sums = [part_sum(2, p, to_up) for p in range(PIECES)]
            self.cross_sums = [part_sum(3, p, to_x) for p in range(PIECES)]

        def always(self):
            return (
                self.ups + self.downs + self.fars
                + [self.own_core, self.down_core, self.up_core] + self.far_core
                + self.pairs + self.far_sums + self.down_sums + self.up_sums
            )

    moves = [[Moves(level, request) for request in range(2)] for level in range(L)]

    loads, stores = [], []

    def load(source, target):
        copy = pltpu.make_async_copy(source, target, local_sems.at[len(loads)])
        copy.start()
        loads.append(copy)
        return copy

    open_loads = [load(tokens, current.at[x]), load(in_gain_hbm, in_gain)]
    pool_loads = [load(owner_hbm, owner), load(slot_hbm, slot), load(pool, pool_in)]
    small_loads = [load(w_beta_hbm, w_beta), load(w_decay_hbm, w_decay)]
    mix_loads = [
        load(source, target)
        for source, target in (
            (conv_query_hbm, conv_query), (conv_key_hbm, conv_key), (conv_value_hbm, conv_value),
            (a_log_hbm, a_log), (dt_bias_hbm, dt_bias), (out_gain_hbm, out_gain),
            (lengths_hbm, lengths),
        )
    ]
    weight_loads, out_loads = [], []
    for level in range(L):
        first = 0
        mine = []
        for source, width in (
            (w_query, DK), (w_key, DK), (w_value, HEADS * DV), (w_gate, HEADS * DV),
        ):
            mine.append(load(source.at[level], weights.at[level, :, pl.ds(first, width)]))
            first += width
        weight_loads.append(mine)
        out_loads.append(load(w_out.at[level], outs.at[level]))

    barrier = pltpu.get_barrier_semaphore()
    partners = [to_x, to_up, to_down, sibling, to_high] + to_z
    for partner in partners:
        pl.semaphore_signal(
            barrier, inc=1, device_id=partner, device_id_type=pl.DeviceIdType.MESH
        )
    pl.semaphore_wait(barrier, len(partners))
    for copy in open_loads:
        copy.wait()

    def spread_piece(level, request, p):
        floats = current[request, piece(p)].astype(F32)
        scale = lax.rsqrt(jnp.mean(floats * floats, -1, keepdims=True) + EPS)
        normed = (floats * scale * in_gain[level : level + 1]).astype(BF)
        buf[level, spot(request, y, core), piece(p)] = normed
        moves[level][request].ups[p].start()
        moves[level][request].downs[p].start()

    def open_request(request):
        move = moves[0][request]
        for p in ORDER:

            @pl.when(x != request)
            def _():
                move.across[p].wait_recv()

            spread_piece(0, request, p)
        move.own_core.start()

    def gather_near(level, request):
        move = moves[level][request]
        for p in ORDER:
            move.ups[p].wait_recv()
            if p < middle:
                move.fars[p].start()
            move.downs[p].wait_recv()
            if p >= middle:
                move.fars[p].start()
        move.down_core.start()
        move.up_core.start()

    def gather_far(level, request):
        move = moves[level][request]
        for first in (0, middle):
            for p in range(first, first + middle):
                move.fars[p].wait_recv()
            move.far_core[first // middle].start()

    def small_weights(level):
        rows = jnp.concatenate(
            [
                w_beta[level].astype(F32),
                w_decay[level].astype(F32),
                jnp.zeros((128 - 2 * HEADS, D), F32),
            ],
            0,
        )
        weights[level, :, WIDE:] = rows.T.astype(BF)

    def keep(request, result, row, rows):
        place = pl.ds(row + PAD, rows)
        q_ref[request, place] = result[:, 0:DK]
        k_ref[request, place] = result[:, DK : 2 * DK]
        v_ref[request, place] = result[:, 2 * DK : 2 * DK + HEADS * DV]
        z_ref[request, pl.ds(row, rows)] = result[:, 2 * DK + HEADS * DV : WIDE]
        raw_ref[request, pl.ds(row, rows)] = result[:, WIDE:]

    def project_chunk(level, request, b):
        rows = buf[level, pl.ds(spot(request, b, 0), 2)].reshape(CHUNK, D)
        result = jnp.dot(rows, weights[level], preferred_element_type=F32)
        keep(request, result, pl.multiple_of(b * CHUNK, CHUNK), CHUNK)

    def project_request(level, request):
        rows = buf[level, pl.ds(request * 8, 8)].reshape(SUF, D)
        result = jnp.dot(rows, weights[level], preferred_element_type=F32)
        keep(request, result, 0, SUF)

    def mix_blocks(level, request):
        blocks = list(range(BLOCKS))
        raws = [
            raw_ref[request, pl.ds(block * CHUNK, CHUNK)].T[0 : 2 * HEADS] for block in blocks
        ]
        block_terms(
            blocks, q_ref.at[request], k_ref.at[request], v_ref.at[request], raws,
            (conv_query[level], conv_key[level], conv_value[level]),
            [a_log[level, head] for head in range(HEADS)],
            [dt_bias[level, head] for head in range(HEADS)],
            lengths[request], move_ref, add_ref, tail_ref,
        )

    def mix_states(level, request):
        holder = owner[request, level]
        near = zbuf[(holder // 2) * SLOTS + slot[request, level]]
        start = jnp.where(holder % 2 == high, near, xland[request * L + level]).astype(F32)

        def store(block, head, rows):
            mixed[pl.ds(block * CHUNK, CHUNK), head * DV : (head + 1) * DV] = rows

        states = run_states(
            start, move_ref, add_ref, tail_ref, z_ref.at[request], out_gain[level : level + 1],
            lengths[request], store,
        )
        for head in range(HEADS):
            final[request, level, head] = states[head]
        stores.append(load(final.at[request, level], final_hbm.at[request, level]))

    def kept(level, request, index, p):
        row = pl.multiple_of(core * ROWS + p * PIECE, PIECE)
        mine = stage[level, request, index, pl.ds(row, PIECE)].astype(F32)
        return mine + sib[level, request, index, piece(p)].astype(F32)

    def scatter_start(level, request):
        move = moves[level][request]

        def term(index, b):
            rows = mixed[pl.ds(pl.multiple_of(b * CHUNK, CHUNK), CHUNK)]
            stage[level, request, index] = jnp.dot(
                rows, outs[level], preferred_element_type=F32
            ).astype(BF)
            move.pairs[index].start()

        def pass_on(index, p, copy):
            sib[level, request, index, piece(p)] = kept(level, request, index, p).astype(BF)
            copy.start()

        term(0, far)
        term(1, down)
        term(2, up)
        move.pairs[0].wait_recv()
        for p in range(middle):
            pass_on(0, p, move.far_sums[p])
            pass_on(0, p + middle, move.far_sums[p + middle])
        term(3, y)
        move.pairs[1].wait_recv()
        move.pairs[2].wait_recv()
        for p in range(middle):
            pass_on(1, p + middle, move.down_sums[p + middle])
            pass_on(2, p, move.up_sums[p])
        move.pairs[3].wait_recv()

    def scatter_middle(level, request):
        move = moves[level][request]
        for step in range(middle):
            for p, index, sums in (
                (step, 1, move.down_sums), (step + middle, 2, move.up_sums),
            ):
                move.far_sums[p].wait_recv()
                total = kept(level, request, index, p)
                total = total + land[level, request, 0, piece(p)].astype(F32)
                sib[level, request, index, piece(p)] = total.astype(BF)
                sums[p].start()

    def scatter_end(level, request):
        move = moves[level][request]
        for p in ORDER:
            move.down_sums[p].wait_recv()
            move.up_sums[p].wait_recv()
            total = kept(level, request, 3, p)
            total = total + land[level, request, 1, piece(p)].astype(F32)
            total = total + land[level, request, 2, piece(p)].astype(F32)
            sib[level, request, 3, piece(p)] = total.astype(BF)
            if level + 1 < L:
                move.cross_sums[p].start()
            else:

                @pl.when(x != request)
                def _():
                    move.cross_sums[p].start()

    def add_piece(level, request, p):
        moves[level][request].cross_sums[p].wait_recv()
        total = sib[level, request, 3, piece(p)].astype(F32)
        total = total + land[level, request, 3, piece(p)].astype(F32)
        old = current[request, piece(p)].astype(F32)
        current[request, piece(p)] = (old + total).astype(BF)

    def next_rows(level, request):
        if level + 1 < L:

            @pl.when(x == request)
            def _():
                for copy in moves[level][request].across:
                    copy.wait_send()

            for p in ORDER:
                add_piece(level, request, p)
                spread_piece(level + 1, request, p)
            moves[level + 1][request].own_core.start()
        else:

            @pl.when(x == request)
            def _():
                for p in ORDER:
                    add_piece(level, request, p)

    for request in range(2):

        @pl.when(x == request)
        def _():
            for p in ORDER:
                moves[0][request].across[p].start()

    open_request(0)

    for copy in pool_loads:
        copy.wait()
    entry_rows = lax.broadcasted_iota(jnp.int32, (8, 128), 0)
    asks = jnp.zeros((8, 128), jnp.int32)
    for entry in range(2 * L):
        row = owner[entry // L, entry % L] * SLOTS + slot[entry // L, entry % L]
        asks = jnp.where(entry_rows == entry, row, asks)
    wanted[...] = asks
    table_copy = remote(wanted, table_in, to_high)
    table_copy.start()
    zbuf[pl.ds(z * SLOTS, SLOTS)] = pool_in[...].astype(BF)
    state_copies = [same(zbuf.at[pl.ds(z * SLOTS, SLOTS)], device) for device in to_z]
    for copy in state_copies[:2]:
        copy.start()
    for ref in (q_ref, k_ref, v_ref):
        ref[:, 0:PAD] = jnp.zeros((2, PAD, ref.shape[2]), F32)
    for copy in small_loads:
        copy.wait()
    small_weights(0)
    for copy in mix_loads:
        copy.wait()
    crossing = [remote(xsend.at[entry], xland.at[entry], to_high) for entry in range(2 * L)]

    def states_across():
        table_copy.wait_recv()
        table_load = load(table_in, table)
        for copy in state_copies:
            copy.wait_recv()
        table_load.wait()
        for entry in range(2 * L):
            asked = table[entry, 0]
            xsend[entry] = zbuf[(asked // (2 * SLOTS)) * SLOTS + asked % SLOTS]
            crossing[entry].start()

    for level in range(L):
        if level:
            small_weights(1)
            scatter_end(0, 0)
            scatter_middle(0, 1)
            next_rows(0, 0)
            scatter_end(0, 1)
        for copy in weight_loads[level]:
            copy.wait()
        move = moves[level][0]
        move.own_core.wait_recv()
        project_chunk(level, 0, y)
        gather_near(level, 0)
        if level:
            next_rows(0, 1)
        else:
            state_copies[2].start()
            open_request(1)
        move.down_core.wait_recv()
        project_chunk(level, 0, down)
        gather_far(level, 0)
        move.up_core.wait_recv()
        project_chunk(level, 0, up)
        for copy in move.far_core:
            copy.wait_recv()
        project_chunk(level, 0, far)
        gather_near(level, 1)
        if level == 0:
            states_across()
        mix_blocks(level, 0)
        gather_far(level, 1)
        if level == 0:
            for copy in crossing:
                copy.wait_recv()
        mix_states(level, 0)
        out_loads[level].wait()
        scatter_start(level, 0)
        move = moves[level][1]
        for copy in [move.own_core, move.down_core, move.up_core] + move.far_core:
            copy.wait_recv()
        project_request(level, 1)
        mix_blocks(level, 1)
        scatter_middle(level, 0)
        mix_states(level, 1)
        scatter_start(level, 1)
    scatter_end(1, 0)
    scatter_middle(1, 1)
    next_rows(1, 0)
    scatter_end(1, 1)
    next_rows(1, 1)
    stores.append(load(current.at[x], out_rows))
    for copy in stores:
        copy.wait()
    for copy in [table_copy] + state_copies + crossing:
        copy.wait_send()
    for level in range(L):
        for request in range(2):
            move = moves[level][request]
            for copy in move.always():
                copy.wait_send()

            if level == 0:
                for copy in move.cross_sums:
                    copy.wait_send()
            else:

                @pl.when(x != request)
                def _():
                    for copy in move.cross_sums:
                        copy.wait_send()


def hand_on_kernel(rows_in, states_in, rows_out, states_out):
    rows_out[...] = rows_in[...]
    states_out[...] = states_in[...]


def hand_on(rows, states):
    vmem = pl.BlockSpec(memory_space=pltpu.VMEM)
    return pl.pallas_call(
        hand_on_kernel,
        name="hand_on",
        in_specs=[vmem, vmem],
        out_specs=[vmem, vmem],
        out_shape=[
            jax.ShapeDtypeStruct(rows.shape, rows.dtype),
            jax.ShapeDtypeStruct(states.shape, states.dtype),
        ],
    )(rows, states)


def run_layers(
    tokens, in_gain, w_query, w_key, w_value, w_gate, w_beta, w_decay,
    conv_query, conv_key, conv_value, a_log, dt_bias, out_gain, w_out,
    pool, owner, slot, lengths,
):
    requests = lengths.shape[0]
    scratch = pltpu.VMEM
    return pl.pallas_call(
        layers_kernel,
        name="layers",
        in_specs=[pl.BlockSpec(memory_space=pl.ANY)] * 19,
        out_specs=[pl.BlockSpec(memory_space=pl.ANY)] * 2,
        out_shape=[
            jax.ShapeDtypeStruct((ROWS, D), BF),
            jax.ShapeDtypeStruct((requests, L, HEADS, DK, DV), F32),
        ],
        scratch_shapes=[
            scratch((L, D, WIDE + 128), BF),
            scratch((L, HEADS * DV, D), BF),
            scratch((L, 16, ROWS, D), BF),
            scratch((2, PAD + SUF, DK), F32),
            scratch((2, PAD + SUF, DK), F32),
            scratch((2, PAD + SUF, HEADS * DV), F32),
            scratch((2, SUF, HEADS * DV), F32),
            scratch((2, SUF, 128), F32),
            scratch((BLOCKS, HEADS, 2 * CHUNK, DK), BF),
            scratch((BLOCKS, HEADS, 2 * CHUNK, DV), F32),
            scratch((BLOCKS, HEADS, 8, DV), F32),
            scratch((SUF, HEADS * DV), BF),
            scratch((L, 2, 4, 2 * ROWS, D), BF),
            scratch((L, 2, 4, ROWS, D), BF),
            scratch((L, 2, 4, ROWS, D), BF),
            scratch((2, ROWS, D), BF),
            scratch((SLOTS, HEADS, DK, DV), F32),
            scratch((4 * SLOTS, HEADS, DK, DV), BF),
            scratch((2 * L, HEADS, DK, DV), BF),
            scratch((2 * L, HEADS, DK, DV), BF),
            scratch((8, 128), jnp.int32),
            scratch((8, 128), jnp.int32),
            pltpu.SMEM((8, 128), jnp.int32),
            scratch((L, D), F32),
            scratch((L, HEADS, D), BF),
            scratch((L, HEADS, D), BF),
            scratch((L, CONV, DK), F32),
            scratch((L, CONV, DK), F32),
            scratch((L, CONV, HEADS * DV), F32),
            scratch((L, DV), F32),
            pltpu.SMEM((L, HEADS), F32),
            pltpu.SMEM((L, HEADS), F32),
            pltpu.SMEM((requests, L), jnp.int32),
            pltpu.SMEM((requests, L), jnp.int32),
            pltpu.SMEM((requests,), jnp.int32),
            scratch((requests, L, HEADS, DK, DV), F32),
            pltpu.SemaphoreType.DMA((SEMS,)),
            pltpu.SemaphoreType.DMA((SEMS,)),
            pltpu.SemaphoreType.DMA((40,)),
        ],
        compiler_params=pltpu.CompilerParams(
            collective_id=0, has_side_effects=True, vmem_limit_bytes=60 * 1024 * 1024
        ),
    )(
        tokens, in_gain, w_query, w_key, w_value, w_gate,
        w_beta.transpose(0, 2, 1), w_decay.transpose(0, 2, 1),
        conv_query, conv_key, conv_value, a_log, dt_bias, out_gain, w_out,
        pool, owner, slot, lengths,
    )


def solution(mesh):
    heads = P(None, None, "head")
    in_specs = (
        P(("req", "head"), None), P(), heads, heads, heads, heads, heads, heads,
        heads, heads, heads, P(None, "head"), P(None, "head"), P(),
        P(None, "head", None), P("req", "head", None, None),
        P("req", None), P("req", None), P("req"),
    )
    out_specs = (P(("req", "head"), None), P("req", None, "head", None, None))

    def on_device(*arrays):
        return tuple(hand_on(*run_layers(*arrays)))

    return jax.shard_map(
        on_device, mesh=mesh, in_specs=in_specs, out_specs=out_specs, check_vma=False
    )
```

```python
import jax
import jax.numpy as jnp
from jax import lax
from jax.experimental import pallas as pl
from jax.experimental.pallas import tpu as pltpu
from jax.sharding import PartitionSpec as P

DK = 128
DV = 128
L = 2
SLOTS = 4
SUF = 512
CONV = 4
HEADS = 2
CHUNK = 128
BLOCKS = SUF // CHUNK
PAD = 8
EPS = 1e-06
BF = jnp.bfloat16
F32 = jnp.float32
D = 2048
ROWS = 64
PIECE = 16
PIECES = ROWS // PIECE
ORDER = (0, 2, 1, 3)
WIDE = 2 * DK + 2 * HEADS * DV
SEMS = 176


def silu(v):
    return v / (1.0 + jnp.exp(-v))


def conv_block(ref, row, width, taps):
    window = ref[pl.ds(row, CHUNK + PAD), 0:width]
    total = None
    for tap in range(CONV):
        first = PAD - (CONV - 1) + tap
        term = window[first : first + CHUNK] * taps[tap : tap + 1]
        total = term if total is None else total + term
    return silu(total)


def unit_rows(vectors):
    return vectors * lax.rsqrt(jnp.sum(vectors * vectors, -1, keepdims=True) + EPS)


def mm(a, b):
    return jnp.dot(a.astype(BF), b.astype(BF), preferred_element_type=F32)


def nt(a, b):
    return lax.dot_general(
        a.astype(BF), b.astype(BF), (((1,), (1,)), ((), ())), preferred_element_type=F32
    )


def lower_inverses(stricts, rows, cols):
    size = 16
    near = rows // size == cols // size
    eye = jnp.where(rows == cols, 1.0, 0.0)
    diags = [jnp.where(near, -strict, 0.0) for strict in stricts]
    inverses = [eye + diag for diag in diags]
    powers = [mm(diag, diag) for diag in diags]
    for _ in range(2):
        both = [
            mm(jnp.concatenate([power, inverse], 0), power)
            for power, inverse in zip(powers, inverses)
        ]
        inverses = [inverse + pair[CHUNK:] for inverse, pair in zip(inverses, both)]
        powers = [pair[:CHUNK] for pair in both]
    inverses = [inverse + mm(inverse, power) for inverse, power in zip(inverses, powers)]
    while size < CHUNK:
        joined = (rows // (2 * size) == cols // (2 * size)) & (rows // size > cols // size)
        halves = [
            mm(jnp.where(joined, strict, 0.0), inverse)
            for strict, inverse in zip(stricts, inverses)
        ]
        inverses = [inverse - mm(inverse, half) for inverse, half in zip(inverses, halves)]
        size *= 2
    return inverses


def gate_rows(raw, a_log, dt_bias, valid):
    rows = []
    for head in range(HEADS):
        rows.append(jnp.where(valid, 1.0 / (1.0 + jnp.exp(-raw[head : head + 1])), 0.0))
    for head in range(HEADS):
        shifted = raw[HEADS + head : HEADS + head + 1] + dt_bias[head]
        soft = jnp.maximum(shifted, 0.0) + jnp.log1p(jnp.exp(-jnp.abs(shifted)))
        rate = jnp.exp(jnp.full((1, CHUNK), a_log[head], F32))
        rows.append(jnp.where(valid, -rate * soft, 0.0))
    rows.append(jnp.zeros((8 - 2 * HEADS, CHUNK), F32))
    return jnp.concatenate(rows, 0)


def block_terms(blocks, q_ref, k_ref, v_ref, raws, taps, a_log, dt_bias, length, move_ref, add_ref, tail_ref):
    rows = lax.broadcasted_iota(jnp.int32, (CHUNK, CHUNK), 0)
    cols = lax.broadcasted_iota(jnp.int32, (CHUNK, CHUNK), 1)
    lane = lax.broadcasted_iota(jnp.int32, (1, CHUNK), 1)
    upper = jnp.where(rows <= cols, 1.0, 0.0)
    gates = [
        gate_rows(raw, a_log, dt_bias, block * CHUNK + lane < length)
        for block, raw in zip(blocks, raws)
    ]
    sums = jnp.dot(
        jnp.concatenate(gates, 0), upper, precision=lax.Precision.HIGHEST, preferred_element_type=F32
    )
    sums = [sums[8 * index : 8 * index + 8] for index in range(len(blocks))]
    columns = [jnp.concatenate([gate, total], 0).T for gate, total in zip(gates, sums)]
    keys = [unit_rows(conv_block(k_ref, block * CHUNK, DK, taps[1])) for block in blocks]
    queries = [
        unit_rows(conv_block(q_ref, block * CHUNK, DK, taps[0])) * DK ** (-0.5) for block in blocks
    ]
    dots = [nt(jnp.concatenate([key, query], 0), key) for key, query in zip(keys, queries)]
    units = [(index, head) for index in range(len(blocks)) for head in range(HEADS)]
    stricts, decays = [], []
    for index, head in units:
        cumul = columns[index][:, 8 + HEADS + head : 9 + HEADS + head]
        cumul_row = sums[index][HEADS + head : HEADS + head + 1]
        decay = jnp.where(rows >= cols, jnp.exp(jnp.minimum(cumul - cumul_row, 0.0)), 0.0)
        beta = columns[index][:, head : head + 1]
        stricts.append(jnp.where(rows > cols, dots[index][:CHUNK] * decay * beta, 0.0))
        decays.append(decay)
    inverses = lower_inverses(stricts, rows, cols)
    values = [conv_block(v_ref, block * CHUNK, HEADS * DV, taps[2]) for block in blocks]
    solved = []
    for (index, head), inverse in zip(units, inverses):
        beta = columns[index][:, head : head + 1]
        grown = jnp.exp(columns[index][:, 8 + HEADS + head : 9 + HEADS + head])
        right = jnp.concatenate(
            [values[index][:, head * DV : (head + 1) * DV] * beta, keys[index] * (beta * grown)], 1
        )
        solved.append(mm(inverse, right))
    for (index, head), decay, solution_now in zip(units, decays, solved):
        cumul = columns[index][:, 8 + HEADS + head : 9 + HEADS + head]
        last = cumul[CHUNK - 1 :]
        key_tail = keys[index] * jnp.exp(last - cumul)
        mixing = dots[index][CHUNK:] * decay
        both = mm(jnp.concatenate([key_tail.T, mixing], 0), solution_now)
        move = jnp.concatenate(
            [-both[:DK, DV:], queries[index] * jnp.exp(cumul) - both[DK:, DV:]], 0
        )
        move_ref[blocks[index], head] = move.astype(BF)
        add_ref[blocks[index], head] = both[:, :DV]
        tail_ref[blocks[index], head] = jnp.broadcast_to(jnp.exp(last), (8, DV))


def run_states(start, move_ref, add_ref, tail_ref, z_ref, gain, length, store):
    states = [start[head] for head in range(HEADS)]
    for block in range(BLOCKS):
        place = block * CHUNK + lax.broadcasted_iota(jnp.int32, (CHUNK, 1), 0)
        valid = (place < length).astype(F32)
        results = [
            mm(move_ref[block, head], states[head]) + add_ref[block, head] for head in range(HEADS)
        ]
        for head in range(HEADS):
            states[head] = tail_ref[block, head][0:1] * states[head] + results[head][:DK]
            out = results[head][DK:]
            scale = lax.rsqrt(jnp.mean(out * out, -1, keepdims=True) + EPS)
            gate = z_ref[pl.ds(block * CHUNK, CHUNK), head * DV : (head + 1) * DV]
            store(block, head, (out * scale * gain * silu(gate) * valid).astype(BF))
    return states


def spot(x, y, core):
    return x * 8 + y * 2 + core


def piece(index):
    return pl.ds(index * PIECE, PIECE)


def layers_kernel(
    tokens, in_gain_hbm, w_query, w_key, w_value, w_gate, w_beta_hbm, w_decay_hbm,
    conv_query_hbm, conv_key_hbm, conv_value_hbm, a_log_hbm, dt_bias_hbm, out_gain_hbm, w_out,
    pool, owner_hbm, slot_hbm, lengths_hbm,
    out_rows, final_hbm,
    weights, outs, buf, q_ref, k_ref, v_ref, z_ref, raw_ref, move_ref, add_ref, tail_ref,
    mixed, stage, sib, land, current, pool_in, zbuf, xsend, xland,
    wanted, table_in, table, in_gain, w_beta, w_decay, conv_query, conv_key, conv_value, out_gain,
    a_log, dt_bias, owner, slot, lengths, final, send_sems, recv_sems, local_sems,
):
    me = lax.axis_index("head")
    group = lax.axis_index("req")
    x, y, core = me // 8, (me // 2) % 4, me % 2
    z, high = group // 2, group % 2
    other, up, down, far = 1 - x, (y + 1) % 4, (y + 3) % 4, (y + 2) % 4
    middle = PIECES // 2

    to_x = {"head": spot(other, y, core)}
    to_up, to_down = {"head": spot(x, up, core)}, {"head": spot(x, down, core)}
    sibling = {"head": spot(x, y, 1 - core)}
    to_high = {"req": z * 2 + 1 - high}
    to_z = [{"req": ((z + step) % 4) * 2 + high} for step in (1, 3, 2)]

    count = [0]

    def remote(source, target, device):
        index = count[0]
        count[0] += 1
        return pltpu.make_async_remote_copy(
            src_ref=source,
            dst_ref=target,
            send_sem=send_sems.at[index],
            recv_sem=recv_sems.at[index],
            device_id=device,
            device_id_type=pl.DeviceIdType.MESH,
        )

    def same(ref, device):
        return remote(ref, ref, device)

    class Moves:
        def __init__(self, level, request):
            def block(b):
                return buf.at[level, spot(request, b, core)]

            def part(b, p):
                return buf.at[level, spot(request, b, core), piece(p)]

            halves = [pl.ds(0, ROWS // 2), pl.ds(ROWS // 2, ROWS // 2)]
            self.across = []
            if level == 0:
                self.across = [same(current.at[request, piece(p)], to_x) for p in range(PIECES)]
            self.ups = [same(part(y, p), to_up) for p in range(PIECES)]
            self.downs = [same(part(y, p), to_down) for p in range(PIECES)]
            self.fars = [
                same(part(down, p), to_up) if p < middle else same(part(up, p), to_down)
                for p in range(PIECES)
            ]
            self.own_core = same(block(y), sibling)
            self.down_core = same(block(down), sibling)
            self.up_core = same(block(up), sibling)
            self.far_core = [
                same(buf.at[level, spot(request, far, core), rows], sibling) for rows in halves
            ]
            here = (level, request)
            theirs = pl.ds(pl.multiple_of((1 - core) * ROWS, ROWS), ROWS)
            self.pairs = [
                remote(stage.at[(*here, index, theirs)], sib.at[(*here, index)], sibling)
                for index in range(4)
            ]

            def part_sum(index, p, device):
                return remote(
                    sib.at[(*here, index, piece(p))], land.at[(*here, index, piece(p))], device
                )

            self.far_sums = [
                part_sum(0, p, to_down if p < middle else to_up) for p in range(PIECES)
            ]
            self.down_sums = [part_sum(1, p, to_down) for p in range(PIECES)]
            self.up_sums = [part_sum(2, p, to_up) for p in range(PIECES)]
            self.cross_sums = [part_sum(3, p, to_x) for p in range(PIECES)]

        def always(self):
            return (
                self.ups + self.downs + self.fars
                + [self.own_core, self.down_core, self.up_core] + self.far_core
                + self.pairs + self.far_sums + self.down_sums + self.up_sums
            )

    moves = [[Moves(level, request) for request in range(2)] for level in range(L)]

    loads, stores = [], []

    def load(source, target):
        copy = pltpu.make_async_copy(source, target, local_sems.at[len(loads)])
        copy.start()
        loads.append(copy)
        return copy

    open_loads = [load(tokens, current.at[x]), load(in_gain_hbm, in_gain)]
    pool_loads = [load(owner_hbm, owner), load(slot_hbm, slot), load(pool, pool_in)]
    small_loads = [load(w_beta_hbm, w_beta), load(w_decay_hbm, w_decay)]
    mix_loads = [
        load(source, target)
        for source, target in (
            (conv_query_hbm, conv_query), (conv_key_hbm, conv_key), (conv_value_hbm, conv_value),
            (a_log_hbm, a_log), (dt_bias_hbm, dt_bias), (out_gain_hbm, out_gain),
            (lengths_hbm, lengths),
        )
    ]
    weight_loads, out_loads = [], []
    for level in range(L):
        first = 0
        mine = []
        for source, width in (
            (w_query, DK), (w_key, DK), (w_value, HEADS * DV), (w_gate, HEADS * DV),
        ):
            mine.append(load(source.at[level], weights.at[level, :, pl.ds(first, width)]))
            first += width
        weight_loads.append(mine)
        out_loads.append(load(w_out.at[level], outs.at[level]))

    barrier = pltpu.get_barrier_semaphore()
    partners = [to_x, to_up, to_down, sibling, to_high] + to_z
    for partner in partners:
        pl.semaphore_signal(
            barrier, inc=1, device_id=partner, device_id_type=pl.DeviceIdType.MESH
        )
    pl.semaphore_wait(barrier, len(partners))
    for copy in open_loads:
        copy.wait()

    def spread_piece(level, request, p):
        floats = current[request, piece(p)].astype(F32)
        scale = lax.rsqrt(jnp.mean(floats * floats, -1, keepdims=True) + EPS)
        normed = (floats * scale * in_gain[level : level + 1]).astype(BF)
        buf[level, spot(request, y, core), piece(p)] = normed
        moves[level][request].ups[p].start()
        moves[level][request].downs[p].start()

    def open_request(request):
        move = moves[0][request]
        for p in ORDER:

            @pl.when(x != request)
            def _():
                move.across[p].wait_recv()

            spread_piece(0, request, p)
        move.own_core.start()

    def gather_near(level, request):
        move = moves[level][request]
        for p in ORDER:
            move.ups[p].wait_recv()
            if p < middle:
                move.fars[p].start()
            move.downs[p].wait_recv()
            if p >= middle:
                move.fars[p].start()
        move.down_core.start()
        move.up_core.start()

    def gather_far(level, request):
        move = moves[level][request]
        for first in (0, middle):
            for p in range(first, first + middle):
                move.fars[p].wait_recv()
            move.far_core[first // middle].start()

    def small_weights(level):
        rows = jnp.concatenate(
            [
                w_beta[level].astype(F32),
                w_decay[level].astype(F32),
                jnp.zeros((128 - 2 * HEADS, D), F32),
            ],
            0,
        )
        weights[level, :, WIDE:] = rows.T.astype(BF)

    def keep(request, result, row, rows):
        place = pl.ds(row + PAD, rows)
        q_ref[request, place] = result[:, 0:DK]
        k_ref[request, place] = result[:, DK : 2 * DK]
        v_ref[request, place] = result[:, 2 * DK : 2 * DK + HEADS * DV]
        z_ref[request, pl.ds(row, rows)] = result[:, 2 * DK + HEADS * DV : WIDE]
        raw_ref[request, pl.ds(row, rows)] = result[:, WIDE:]

    def project_chunk(level, request, b):
        rows = buf[level, pl.ds(spot(request, b, 0), 2)].reshape(CHUNK, D)
        result = jnp.dot(rows, weights[level], preferred_element_type=F32)
        keep(request, result, pl.multiple_of(b * CHUNK, CHUNK), CHUNK)

    def project_request(level, request):
        rows = buf[level, pl.ds(request * 8, 8)].reshape(SUF, D)
        result = jnp.dot(rows, weights[level], preferred_element_type=F32)
        keep(request, result, 0, SUF)

    def mix_blocks(level, request):
        blocks = list(range(BLOCKS))
        raws = [
            raw_ref[request, pl.ds(block * CHUNK, CHUNK)].T[0 : 2 * HEADS] for block in blocks
        ]
        block_terms(
            blocks, q_ref.at[request], k_ref.at[request], v_ref.at[request], raws,
            (conv_query[level], conv_key[level], conv_value[level]),
            [a_log[level, head] for head in range(HEADS)],
            [dt_bias[level, head] for head in range(HEADS)],
            lengths[request], move_ref, add_ref, tail_ref,
        )

    def mix_states(level, request):
        holder = owner[request, level]
        near = zbuf[(holder // 2) * SLOTS + slot[request, level]]
        start = jnp.where(holder % 2 == high, near, xland[request * L + level]).astype(F32)

        def store(block, head, rows):
            mixed[pl.ds(block * CHUNK, CHUNK), head * DV : (head + 1) * DV] = rows

        states = run_states(
            start, move_ref, add_ref, tail_ref, z_ref.at[request], out_gain[level : level + 1],
            lengths[request], store,
        )
        for head in range(HEADS):
            final[request, level, head] = states[head]
        stores.append(load(final.at[request, level], final_hbm.at[request, level]))

    def kept(level, request, index, p):
        row = pl.multiple_of(core * ROWS + p * PIECE, PIECE)
        mine = stage[level, request, index, pl.ds(row, PIECE)].astype(F32)
        return mine + sib[level, request, index, piece(p)].astype(F32)

    def scatter_start(level, request):
        move = moves[level][request]

        def term(index, b):
            rows = mixed[pl.ds(pl.multiple_of(b * CHUNK, CHUNK), CHUNK)]
            stage[level, request, index] = jnp.dot(
                rows, outs[level], preferred_element_type=F32
            ).astype(BF)
            move.pairs[index].start()

        def pass_on(index, p, copy):
            sib[level, request, index, piece(p)] = kept(level, request, index, p).astype(BF)
            copy.start()

        term(0, far)
        term(1, down)
        term(2, up)
        move.pairs[0].wait_recv()
        for p in range(middle):
            pass_on(0, p, move.far_sums[p])
            pass_on(0, p + middle, move.far_sums[p + middle])
        term(3, y)
        move.pairs[1].wait_recv()
        move.pairs[2].wait_recv()
        for p in range(middle):
            pass_on(1, p + middle, move.down_sums[p + middle])
            pass_on(2, p, move.up_sums[p])
    def scatter_middle(level, request):
        move = moves[level][request]
        for step in range(middle):
            for p, index, sums in (
                (step, 1, move.down_sums), (step + middle, 2, move.up_sums),
            ):
                move.far_sums[p].wait_recv()
                total = kept(level, request, index, p)
                total = total + land[level, request, 0, piece(p)].astype(F32)
                sib[level, request, index, piece(p)] = total.astype(BF)
                sums[p].start()

    def scatter_end(level, request):
        move = moves[level][request]
        move.pairs[3].wait_recv()
        for p in ORDER:
            move.down_sums[p].wait_recv()
            move.up_sums[p].wait_recv()
            total = kept(level, request, 3, p)
            total = total + land[level, request, 1, piece(p)].astype(F32)
            total = total + land[level, request, 2, piece(p)].astype(F32)
            sib[level, request, 3, piece(p)] = total.astype(BF)
            if level + 1 < L:
                move.cross_sums[p].start()
            else:

                @pl.when(x != request)
                def _():
                    move.cross_sums[p].start()

    def add_piece(level, request, p):
        moves[level][request].cross_sums[p].wait_recv()
        total = sib[level, request, 3, piece(p)].astype(F32)
        total = total + land[level, request, 3, piece(p)].astype(F32)
        old = current[request, piece(p)].astype(F32)
        current[request, piece(p)] = (old + total).astype(BF)

    def next_rows(level, request):
        if level + 1 < L:

            @pl.when(x == request)
            def _():
                for copy in moves[level][request].across:
                    copy.wait_send()

            for p in ORDER:
                add_piece(level, request, p)
                spread_piece(level + 1, request, p)
            moves[level + 1][request].own_core.start()
        else:

            @pl.when(x == request)
            def _():
                for p in ORDER:
                    add_piece(level, request, p)

    for request in range(2):

        @pl.when(x == request)
        def _():
            for p in ORDER:
                moves[0][request].across[p].start()

    open_request(0)

    for copy in pool_loads:
        copy.wait()
    entry_rows = lax.broadcasted_iota(jnp.int32, (8, 128), 0)
    asks = jnp.zeros((8, 128), jnp.int32)
    for entry in range(2 * L):
        row = owner[entry // L, entry % L] * SLOTS + slot[entry // L, entry % L]
        asks = jnp.where(entry_rows == entry, row, asks)
    wanted[...] = asks
    table_copy = remote(wanted, table_in, to_high)
    table_copy.start()
    zbuf[pl.ds(z * SLOTS, SLOTS)] = pool_in[...].astype(BF)
    state_copies = [same(zbuf.at[pl.ds(z * SLOTS, SLOTS)], device) for device in to_z]
    for copy in state_copies[:2]:
        copy.start()
    for ref in (q_ref, k_ref, v_ref):
        ref[:, 0:PAD] = jnp.zeros((2, PAD, ref.shape[2]), F32)
    for copy in small_loads:
        copy.wait()
    small_weights(0)
    for copy in mix_loads:
        copy.wait()
    crossing = [remote(xsend.at[entry], xland.at[entry], to_high) for entry in range(2 * L)]

    def states_across():
        table_copy.wait_recv()
        table_load = load(table_in, table)
        for copy in state_copies:
            copy.wait_recv()
        table_load.wait()
        for entry in range(2 * L):
            asked = table[entry, 0]
            xsend[entry] = zbuf[(asked // (2 * SLOTS)) * SLOTS + asked % SLOTS]
            crossing[entry].start()

    for level in range(L):
        if level:
            small_weights(1)
            scatter_end(0, 0)
            scatter_middle(0, 1)
            next_rows(0, 0)
            scatter_end(0, 1)
        for copy in weight_loads[level]:
            copy.wait()
        move = moves[level][0]
        move.own_core.wait_recv()
        project_chunk(level, 0, y)
        gather_near(level, 0)
        if level:
            next_rows(0, 1)
        else:
            state_copies[2].start()
            open_request(1)
        move.down_core.wait_recv()
        project_chunk(level, 0, down)
        gather_far(level, 0)
        move.up_core.wait_recv()
        project_chunk(level, 0, up)
        for copy in move.far_core:
            copy.wait_recv()
        project_chunk(level, 0, far)
        gather_near(level, 1)
        if level == 0:
            states_across()
        mix_blocks(level, 0)
        gather_far(level, 1)
        if level == 0:
            for copy in crossing:
                copy.wait_recv()
        mix_states(level, 0)
        out_loads[level].wait()
        scatter_start(level, 0)
        move = moves[level][1]
        for copy in [move.own_core, move.down_core, move.up_core] + move.far_core:
            copy.wait_recv()
        project_request(level, 1)
        mix_blocks(level, 1)
        scatter_middle(level, 0)
        mix_states(level, 1)
        scatter_start(level, 1)
    scatter_end(1, 0)
    scatter_middle(1, 1)
    scatter_end(1, 1)
    next_rows(1, 0)
    next_rows(1, 1)
    stores.append(load(current.at[x], out_rows))
    for copy in stores:
        copy.wait()
    for copy in [table_copy] + state_copies + crossing:
        copy.wait_send()
    for level in range(L):
        for request in range(2):
            move = moves[level][request]
            for copy in move.always():
                copy.wait_send()

            if level == 0:
                for copy in move.cross_sums:
                    copy.wait_send()
            else:

                @pl.when(x != request)
                def _():
                    for copy in move.cross_sums:
                        copy.wait_send()


def hand_on_kernel(rows_in, states_in, rows_out, states_out):
    rows_out[...] = rows_in[...]
    states_out[...] = states_in[...]


def hand_on(rows, states):
    vmem = pl.BlockSpec(memory_space=pltpu.VMEM)
    return pl.pallas_call(
        hand_on_kernel,
        name="hand_on",
        in_specs=[vmem, vmem],
        out_specs=[vmem, vmem],
        out_shape=[
            jax.ShapeDtypeStruct(rows.shape, rows.dtype),
            jax.ShapeDtypeStruct(states.shape, states.dtype),
        ],
    )(rows, states)


def run_layers(
    tokens, in_gain, w_query, w_key, w_value, w_gate, w_beta, w_decay,
    conv_query, conv_key, conv_value, a_log, dt_bias, out_gain, w_out,
    pool, owner, slot, lengths,
):
    requests = lengths.shape[0]
    scratch = pltpu.VMEM
    return pl.pallas_call(
        layers_kernel,
        name="layers",
        in_specs=[pl.BlockSpec(memory_space=pl.ANY)] * 19,
        out_specs=[pl.BlockSpec(memory_space=pl.ANY)] * 2,
        out_shape=[
            jax.ShapeDtypeStruct((ROWS, D), BF),
            jax.ShapeDtypeStruct((requests, L, HEADS, DK, DV), F32),
        ],
        scratch_shapes=[
            scratch((L, D, WIDE + 128), BF),
            scratch((L, HEADS * DV, D), BF),
            scratch((L, 16, ROWS, D), BF),
            scratch((2, PAD + SUF, DK), F32),
            scratch((2, PAD + SUF, DK), F32),
            scratch((2, PAD + SUF, HEADS * DV), F32),
            scratch((2, SUF, HEADS * DV), F32),
            scratch((2, SUF, 128), F32),
            scratch((BLOCKS, HEADS, 2 * CHUNK, DK), BF),
            scratch((BLOCKS, HEADS, 2 * CHUNK, DV), F32),
            scratch((BLOCKS, HEADS, 8, DV), F32),
            scratch((SUF, HEADS * DV), BF),
            scratch((L, 2, 4, 2 * ROWS, D), BF),
            scratch((L, 2, 4, ROWS, D), BF),
            scratch((L, 2, 4, ROWS, D), BF),
            scratch((2, ROWS, D), BF),
            scratch((SLOTS, HEADS, DK, DV), F32),
            scratch((4 * SLOTS, HEADS, DK, DV), BF),
            scratch((2 * L, HEADS, DK, DV), BF),
            scratch((2 * L, HEADS, DK, DV), BF),
            scratch((8, 128), jnp.int32),
            scratch((8, 128), jnp.int32),
            pltpu.SMEM((8, 128), jnp.int32),
            scratch((L, D), F32),
            scratch((L, HEADS, D), BF),
            scratch((L, HEADS, D), BF),
            scratch((L, CONV, DK), F32),
            scratch((L, CONV, DK), F32),
            scratch((L, CONV, HEADS * DV), F32),
            scratch((L, DV), F32),
            pltpu.SMEM((L, HEADS), F32),
            pltpu.SMEM((L, HEADS), F32),
            pltpu.SMEM((requests, L), jnp.int32),
            pltpu.SMEM((requests, L), jnp.int32),
            pltpu.SMEM((requests,), jnp.int32),
            scratch((requests, L, HEADS, DK, DV), F32),
            pltpu.SemaphoreType.DMA((SEMS,)),
            pltpu.SemaphoreType.DMA((SEMS,)),
            pltpu.SemaphoreType.DMA((40,)),
        ],
        compiler_params=pltpu.CompilerParams(
            collective_id=0, has_side_effects=True, vmem_limit_bytes=60 * 1024 * 1024
        ),
    )(
        tokens, in_gain, w_query, w_key, w_value, w_gate,
        w_beta.transpose(0, 2, 1), w_decay.transpose(0, 2, 1),
        conv_query, conv_key, conv_value, a_log, dt_bias, out_gain, w_out,
        pool, owner, slot, lengths,
    )


def solution(mesh):
    heads = P(None, None, "head")
    in_specs = (
        P(("req", "head"), None), P(), heads, heads, heads, heads, heads, heads,
        heads, heads, heads, P(None, "head"), P(None, "head"), P(),
        P(None, "head", None), P("req", "head", None, None),
        P("req", None), P("req", None), P("req"),
    )
    out_specs = (P(("req", "head"), None), P("req", None, "head", None, None))

    def on_device(*arrays):
        return tuple(hand_on(*run_layers(*arrays)))

    return jax.shard_map(
        on_device, mesh=mesh, in_specs=in_specs, out_specs=out_specs, check_vma=False
    )
```
